32 devices in a mesh: dp: 8 (over y, x, core), mp: 4 (over z).
Axes of the slice: x: 2, y: 2, z: 4, core: 2. Of those that a mesh axis runs over, the one named last changes fastest.
Arguments:
- response_query: bfloat16 [384, 8, 6144], P('dp', None, 'mp'), may hold values from -80 to 80, as said below
- response_keys: bfloat16 [2, 384, 8, 768], P(None, 'dp'), may hold values from -8 to 8
- prompt_cache: bfloat16 [2, 8, 1024, 768], P(None, 'dp'), may hold values from -6 to 6
- lengths: int32 [384], P('dp'), may hold values from 1 to 8, as said below
- owners: int32 [384], P('dp'), may hold values from 0 to 7, as said below
- pairing: int32 [384], replicated, may hold values from 0 to 383, each once
- residual: bfloat16 [384, 8192], P(None, 'dp'), may hold values from -90 to 90
- output_weight: bfloat16 [6144, 8192], P('mp', 'dp'), may hold values from -0.3125 to 0.3125
- norm_gain: float32 [8192], P('dp'), may hold values from 0.1 to 1.9
- reward_head: float32 [8192], P('dp'), may hold values from -0.0625 to 0.0625
Outputs:
- attention_rows: bfloat16 [384, 8, 6144], P('dp', None, 'mp')
- rewards: float32 [384], replicated
- pair_loss: float32 [], replicated
- weight_gradient: float32 [6144, 8192], P('mp', 'dp')
- head_gradient: float32 [8192], P('dp')
- pooled_gradient: float32 [384, 6144], P('dp', 'mp')
The draws below stay inside these ranges and needn't reach their ends.
Inputs may be any that keep to these rules, and one draw needn't show every extreme that they name: `response_query`: drawn jointly with response_keys. `lengths`: every dp index holds a response of length 8. The responses of one dp index spread over owners as evenly as possible: each owner receives at most 6 of them, and some owner receives exactly 6.
All inputs are finite; a program needn't handle non-finite values.
Results may differ from the reference program's by a relative error of at most 0.0056.
Values may be sent and summed in bfloat16 or wider, within the bound.
A program may use at most 64 MiB of HBM per device.

```python
import math
import jax
import jax.numpy as jnp
from jax import lax

D = 8192
HD = 128
Q_HEADS = 48
KV_HEADS = 6
SLOT = 8
RESP_DEV = 48
PREFIX = 1024
RESPONSES = 384
N_DP = 8


def query_and_keys(key):
    first, second = jax.random.split(jax.random.fold_in(key, 11), 2)
    queries = jnp.clip(jax.random.normal(first, (RESPONSES, SLOT, Q_HEADS, HD)), -6.0, 6.0)
    keys_values = jnp.clip(jax.random.normal(second, (2, RESPONSES, SLOT, KV_HEADS, HD)), -6.0, 6.0)
    return (queries.reshape(RESPONSES, SLOT, Q_HEADS * HD), keys_values.reshape(2, RESPONSES, SLOT, KV_HEADS * HD))


def draw_response_query(key, part):
    return query_and_keys(key)[0].astype(jnp.bfloat16)


def draw_response_keys(key, part):
    return query_and_keys(key)[1].astype(jnp.bfloat16)


def draw_lengths(key, part):
    devices = RESPONSES // RESP_DEV
    base = jax.random.randint(key, (devices, RESP_DEV), 1, SLOT + 1)
    longest = jax.random.randint(jax.random.fold_in(key, 7), (devices,), 0, RESP_DEV)
    hits = jnp.arange(RESP_DEV)[None, :] == longest[:, None]
    return jnp.where(hits, SLOT, base).reshape(RESPONSES).astype(jnp.int32)


def draw_owners(key, part):
    devices = RESPONSES // RESP_DEV
    device_keys = jax.random.split(jax.random.fold_in(key, 5), devices)
    orders = jax.vmap(lambda single: jax.random.permutation(single, devices))(device_keys)
    columns = jnp.arange(RESP_DEV) % devices
    return orders[:, columns].reshape(RESPONSES).astype(jnp.int32)


def draw_residual(key, part):
    first, second, third = jax.random.split(jax.random.fold_in(key, 3), 3)
    row_scale = jnp.exp(jax.random.uniform(first, (RESPONSES, 1), minval=math.log(0.5), maxval=math.log(5.0)))
    column_scale = jnp.exp(jax.random.uniform(second, (1, D), minval=math.log(0.3), maxval=math.log(3.0)))
    base = jnp.clip(jax.random.normal(third, (RESPONSES, D)), -6.0, 6.0)
    return (base * row_scale * column_scale).astype(jnp.bfloat16)


def steps_of(stream_key, dims, shards, low, high):
    level, own = 1.0, jax.random.fold_in(stream_key, 6)
    for axis_at, blocks in shards:
        heights = jnp.exp(jax.random.uniform(jax.random.fold_in(own, axis_at), (blocks,), jnp.float32, low / len(shards), high / len(shards)))
        level = level * jnp.repeat(heights, dims[axis_at] // blocks).reshape([-1 if axis == axis_at else 1 for axis in range(len(dims))])
    return level


def scatter_about(own_key, shape, scale, most, shards=(), dtype=jnp.bfloat16):
    values = scale * jax.random.normal(own_key, shape, jnp.float32)
    if shards:
        values = values * steps_of(own_key, shape, shards, -0.22, 0.18)
    return jnp.clip(values, -most, most).astype(dtype)


def setup_inputs(seed: int = 0) -> dict:
    keys = jax.random.split(jax.random.key(seed), 11)
    response_query = draw_response_query(jax.random.fold_in(keys[10], 71), 0)
    response_keys = draw_response_keys(jax.random.fold_in(keys[10], 71), 0)
    prompt_cache = scatter_about(keys[2], (2, N_DP, PREFIX, KV_HEADS * HD), 1.0, 6.0, ((1, 8),))
    lengths = draw_lengths(jax.random.fold_in(keys[10], 71), 0)
    owners = draw_owners(jax.random.fold_in(keys[10], 71), 0)
    pairing = jax.random.permutation(keys[5], RESPONSES).astype(jnp.int32)
    residual = draw_residual(jax.random.fold_in(keys[10], 71), 0)
    output_weight = scatter_about(keys[7], (Q_HEADS * HD, D), (Q_HEADS * HD // 16) ** -0.5, 0.3125, ((0, 4), (1, 8)))
    norm_gain = jnp.clip(1.0 + 0.18 * jax.random.normal(keys[8], (D,), jnp.float32), 0.1, 1.9)
    reward_head = scatter_about(keys[9], (D,), D ** -0.5, 0.0625, ((0, 8),), jnp.float32)
    return {"response_query": response_query, "response_keys": response_keys, "prompt_cache": prompt_cache, "lengths": lengths, "owners": owners, "pairing": pairing, "residual": residual, "output_weight": output_weight, "norm_gain": norm_gain, "reward_head": reward_head}


EPSILON = 1e-05

def bradley_terry(rewards, pairing):
    chosen = pairing[0::2]
    rejected = pairing[1::2]
    margin = rewards[chosen] - rewards[rejected]
    loss_value = jnp.mean(jax.nn.softplus(-margin))
    slope = -jax.nn.sigmoid(-margin) / margin.shape[0]
    reward_slope = jnp.zeros_like(rewards).at[chosen].add(slope).at[rejected].add(-slope)
    return (loss_value, reward_slope)

def round_weights(values):
    return lax.optimization_barrier(values.astype(jnp.bfloat16)).astype(jnp.float32)

def reference(response_query, response_keys, prompt_cache, lengths, owners, pairing, residual, output_weight, norm_gain, reward_head):
    score_scale = 1.0 / math.sqrt(HD)
    group_size = Q_HEADS // KV_HEADS
    offsets = jnp.arange(SLOT)

    def attend(item):
        query_rows, key_rows, length, owner_index = item
        prompt = lax.dynamic_index_in_dim(prompt_cache, owner_index, axis=1, keepdims=False)
        queries = query_rows.reshape(SLOT, KV_HEADS, group_size, HD).astype(jnp.float32)
        cache_keys = prompt[0].reshape(PREFIX, KV_HEADS, HD).astype(jnp.float32)
        cache_values = prompt[1].reshape(PREFIX, KV_HEADS, HD).astype(jnp.float32)
        own_keys = key_rows[0].reshape(SLOT, KV_HEADS, HD).astype(jnp.float32)
        own_values = key_rows[1].reshape(SLOT, KV_HEADS, HD).astype(jnp.float32)
        far_scores = jnp.einsum('tkgh,pkh->kgtp', queries, cache_keys) * score_scale
        near_scores = jnp.einsum('tkgh,skh->kgts', queries, own_keys) * score_scale
        allowed = (offsets[None, :] <= offsets[:, None]) & (offsets[None, :] < length)
        near_scores = jnp.where(allowed[None, None], near_scores, -jnp.inf)
        row_top = jnp.maximum(lax.optimization_barrier(jnp.max(far_scores, axis=-1)), lax.optimization_barrier(jnp.max(near_scores, axis=-1)))
        far_weight = jnp.exp(far_scores - row_top[..., None])
        near_weight = jnp.exp(near_scores - row_top[..., None])
        weight_total = lax.optimization_barrier(jnp.sum(far_weight, axis=-1)) + lax.optimization_barrier(jnp.sum(near_weight, axis=-1))
        output = jnp.einsum('kgtp,pkh->tkgh', round_weights(far_weight), cache_values)
        output = output + jnp.einsum('kgts,skh->tkgh', round_weights(near_weight), own_values)
        output = output / jnp.transpose(weight_total, (2, 0, 1))[..., None]
        output = jnp.where((offsets < length)[:, None, None, None], output, 0.0)
        return output.reshape(SLOT, Q_HEADS * HD).astype(jnp.bfloat16)
    attention_rows = lax.map(attend, (response_query, jnp.moveaxis(response_keys, 1, 0), lengths, owners))
    pooled = attention_rows[jnp.arange(RESPONSES), lengths - 1]
    combined = jnp.dot(pooled, output_weight, preferred_element_type=jnp.float32) + residual.astype(jnp.float32)
    scaled_head = norm_gain * reward_head
    square_sum = lax.optimization_barrier(jnp.sum(combined * combined, axis=1))
    signal = lax.optimization_barrier(jnp.sum(combined * scaled_head[None, :], axis=1))
    inverse = lax.rsqrt(square_sum / D + EPSILON)
    rewards = inverse * signal
    pair_loss, reward_slope = bradley_terry(rewards, pairing)
    direct_term = reward_slope * inverse
    norm_term = reward_slope * inverse * inverse * inverse * signal / D
    upstream = direct_term[:, None] * scaled_head[None, :] - norm_term[:, None] * combined
    upstream_half = upstream.astype(jnp.bfloat16)
    head_gradient = lax.optimization_barrier(jnp.sum(direct_term[:, None] * combined * norm_gain[None, :], axis=0))
    weight_gradient = jnp.dot(pooled.T, upstream_half, preferred_element_type=jnp.float32)
    pooled_gradient = jnp.dot(upstream_half, output_weight.T, preferred_element_type=jnp.float32)
    return (attention_rows, rewards, pair_loss, weight_gradient, head_gradient, pooled_gradient)
```

```python
import functools
import math

import jax
import jax.numpy as jnp
from jax import lax
from jax.experimental import pallas as pl
from jax.experimental.pallas import tpu as pltpu
from jax.sharding import PartitionSpec as P

D = 8192
HD = 128
Q_HEADS = 48
KV_HEADS = 6


EPSILON = 1e-05


def bradley_terry(rewards, pairing):
    count = rewards.shape[0]
    chosen = pairing[0::2, None] == jnp.arange(count)[None, :]
    rejected = pairing[1::2, None] == jnp.arange(count)[None, :]
    sign = chosen.astype(jnp.float32) - rejected.astype(jnp.float32)
    margin = jnp.sum(sign * rewards[None, :], axis=1)
    loss_value = jnp.mean(jax.nn.softplus(-margin))
    slope = -jax.nn.sigmoid(-margin) / margin.shape[0]
    reward_slope = jnp.sum(sign * slope[:, None], axis=0)
    return (loss_value, reward_slope)


def pack_kernel(window, meta, query, keys, out, late):
    slots = out.shape[0]
    rest = late.shape[2]
    width = query.shape[2] - rest
    span = window * HD
    first = pl.multiple_of(meta[2 * slots] * HD, HD)

    def body(p, carry):
        r = meta[p]
        out[p, :, pl.ds(0, width)] = query[r, :, pl.ds(0, width)]
        late[p] = query[r, :, pl.ds(width, rest)]
        out[p, :, pl.ds(width, span)] = keys[0, r, :, pl.ds(first, span)]
        out[p, :, pl.ds(width + span, span)] = keys[1, r, :, pl.ds(first, span)]
        length = meta[slots + p].astype(jnp.float32)
        place = r.astype(jnp.float32)
        lane = lax.broadcasted_iota(jnp.int32, (out.shape[1], HD), 1)
        out[p, :, pl.ds(width + 2 * span, HD)] = jnp.where(lane < HD // 2, length, place).astype(
            jnp.bfloat16
        )
        return carry

    lax.fori_loop(0, slots, body, 0)


def attention_kernel(slot_count, placed, meta, query, own_k, own_v, lens, cache, out, pooled):
    rows = query.shape[0]
    head = pl.program_id(0)
    chunk = 128
    blocks = chunk // slot_count
    scale = math.log2(math.e) / math.sqrt(HD)
    contract = (((1,), (1,)), ((), ()))
    row = lax.broadcasted_iota(jnp.int32, (chunk, chunk), 0)
    col = lax.broadcasted_iota(jnp.int32, (chunk, chunk), 1)
    t = row % slot_count
    s = col % slot_count
    causal = (row // slot_count == col // slot_count) & (s <= t)
    s_float = s.astype(jnp.float32)
    t_float = t.astype(jnp.float32)
    gather = lax.broadcasted_iota(jnp.int32, (blocks, chunk), 0)
    member = lax.broadcasted_iota(jnp.int32, (blocks, chunk), 1)
    gather = jnp.where(gather == member // slot_count, 1.0, 0.0).astype(jnp.bfloat16)
    for start in range(0, rows, chunk):
        here = pl.ds(start, chunk)
        q = query[here, :]
        length = jnp.broadcast_to(lens[here, :].astype(jnp.float32)[:, 0:1], (chunk, chunk))
        far = lax.dot_general(q, cache[0, 0], contract, preferred_element_type=jnp.float32)
        near = lax.dot_general(q, own_k[here, :], contract, preferred_element_type=jnp.float32)
        near = jnp.where(causal & (s_float < length), near, -jnp.inf)
        top = jnp.maximum(
            jnp.max(far, axis=1, keepdims=True), jnp.max(near, axis=1, keepdims=True)
        )
        far = jnp.exp2((far - top) * scale)
        near = jnp.exp2((near - top) * scale)
        total = jnp.sum(far, axis=1, keepdims=True) + jnp.sum(near, axis=1, keepdims=True)
        value = jnp.dot(far.astype(jnp.bfloat16), cache[1, 0], preferred_element_type=jnp.float32)
        value += jnp.dot(
            near.astype(jnp.bfloat16), own_v[here, :], preferred_element_type=jnp.float32
        )
        value = jnp.where(t_float < length, value / total, 0.0)
        out[here, :] = value.astype(jnp.bfloat16)
        last = jnp.where(t_float == length - 1.0, value, 0.0)
        last = jnp.dot(gather, last.astype(jnp.bfloat16), preferred_element_type=jnp.float32)
        there = pl.ds(start // slot_count, blocks)
        pooled[there, pl.ds(pl.multiple_of(head * HD, HD), HD)] = last.astype(jnp.bfloat16)

        if placed:

            @pl.when(head == 0)
            def _():
                place = lens[here, :].astype(jnp.float32).reshape(blocks, slot_count, HD)
                pooled[there, pl.ds(pooled.shape[1] - HD, HD)] = jnp.max(place, axis=1).astype(
                    jnp.bfloat16
                )


def unpack_kernel(meta, returned, out):
    def body(r, carry):
        out[r] = returned[meta[r]]
        return carry

    lax.fori_loop(0, out.shape[0], body, 0)


def stepwise_shards(
    response_query,
    response_keys,
    prompt_cache,
    lengths,
    owners,
    pairing,
    residual,
    output_weight,
    norm_gain,
    reward_head,
):
    groups = lax.axis_size("dp")
    planes = lax.axis_size("mp")
    model_rank = lax.axis_index("mp")
    held_count, slot_count, head_width = response_query.shape
    local_heads = head_width // HD
    group_size = Q_HEADS // KV_HEADS
    per_owner = (held_count + groups - 1) // groups
    capacity = groups * per_owner
    window = max(
        (m * local_heads + local_heads - 1) // group_size - m * local_heads // group_size + 1
        for m in range(planes)
    )
    first_head = jnp.minimum(model_rank * local_heads // group_size, KV_HEADS - window)
    head_kv = (model_rank * local_heads + jnp.arange(local_heads)) // group_size
    positions = jnp.arange(held_count)
    earlier = (owners[None, :] == owners[:, None]) & (positions[None, :] < positions[:, None])
    target = (owners * per_owner + jnp.sum(earlier, axis=1)).astype(jnp.int32)
    sent_from = (target[None, :] == jnp.arange(capacity)[:, None]).astype(jnp.int32)
    source = jnp.sum(sent_from * positions[None, :], axis=1)
    slot_length = jnp.sum(sent_from * lengths[None, :], axis=1)
    params = pltpu.CompilerParams(vmem_limit_bytes=40 * 1024 * 1024)
    vmem = pl.BlockSpec(memory_space=pltpu.VMEM)
    smem = pl.BlockSpec(memory_space=pltpu.SMEM)
    early = local_heads - local_heads // 2
    late_width = local_heads // 2 * HD
    packed_width = early * HD + (2 * window + 1) * HD
    packed, late = pl.pallas_call(
        functools.partial(pack_kernel, window),
        out_shape=(
            jax.ShapeDtypeStruct((capacity, slot_count, packed_width), jnp.bfloat16),
            jax.ShapeDtypeStruct((capacity, slot_count, late_width), jnp.bfloat16),
        ),
        in_specs=[smem, vmem, vmem],
        out_specs=(vmem, vmem),
        compiler_params=params,
        name="pack",
    )(
        jnp.concatenate([source, slot_length, first_head[None]]).astype(jnp.int32),
        response_query,
        response_keys,
    )
    packed = packed.reshape(groups, per_owner, slot_count, packed_width)
    arrived = lax.all_to_all(packed, "dp", split_axis=0, concat_axis=0, tiled=True)
    late = late.reshape(groups, per_owner, slot_count, late_width)
    late = lax.all_to_all(late, "dp", split_axis=0, concat_axis=0, tiled=True)
    rows = capacity * slot_count
    late = late.reshape(rows, late_width)
    arrived = arrived.reshape(rows, packed_width)
    block = (rows, HD)

    def attend(query, head_base, heads, placed):
        pooled_width = (heads + placed) * HD
        at = lambda meta, h: meta[local_heads + head_base + h]
        return pl.pallas_call(
            functools.partial(attention_kernel, slot_count, placed),
            out_shape=(
                jax.ShapeDtypeStruct((rows, heads * HD), jnp.bfloat16),
                jax.ShapeDtypeStruct((capacity, pooled_width), jnp.bfloat16),
            ),
            grid_spec=pltpu.PrefetchScalarGridSpec(
                num_scalar_prefetch=1,
                grid=(heads,),
                in_specs=[
                    pl.BlockSpec(block, lambda h, meta: (0, h)),
                    pl.BlockSpec(block, lambda h, meta: (0, early + at(meta, h))),
                    pl.BlockSpec(block, lambda h, meta: (0, early + window + at(meta, h))),
                    pl.BlockSpec(block, lambda h, meta: (0, early + 2 * window)),
                    pl.BlockSpec(
                        (2, 1, prompt_cache.shape[2], HD),
                        lambda h, meta: (0, 0, 0, meta[head_base + h]),
                    ),
                ],
                out_specs=(
                    pl.BlockSpec(block, lambda h, meta: (0, h)),
                    pl.BlockSpec((capacity, pooled_width), lambda h, meta: (0, 0)),
                ),
            ),
            compiler_params=params,
            cost_estimate=pl.CostEstimate(
                flops=4 * rows * heads * HD * prompt_cache.shape[2],
                bytes_accessed=8 * rows * heads * HD,
                transcendentals=rows * heads * prompt_cache.shape[2],
            ),
            name="attention_early" if placed else "attention_late",
        )(
            jnp.concatenate([head_kv, head_kv - first_head]).astype(jnp.int32),
            query,
            arrived,
            arrived,
            arrived,
            prompt_cache,
        )

    def share_rows(own):
        copies = jnp.broadcast_to(own[None], (groups,) + own.shape)
        copies = lax.all_to_all(copies, "dp", split_axis=0, concat_axis=0, tiled=True)
        return copies.reshape(groups * own.shape[0], own.shape[1])

    attended_early, pooled_early = attend(arrived, 0, early, True)
    pooled_slots = share_rows(pooled_early)
    attended_late, pooled_late = attend(late, early, local_heads - early, False)
    pooled_late = share_rows(pooled_late)
    attended = jnp.concatenate([attended_early, attended_late], axis=1)
    result = attended.reshape(groups, per_owner, slot_count, head_width)
    returned = lax.all_to_all(result, "dp", split_axis=0, concat_axis=0, tiled=True)
    attention_rows = pl.pallas_call(
        unpack_kernel,
        out_shape=jax.ShapeDtypeStruct(response_query.shape, jnp.bfloat16),
        in_specs=[smem, vmem],
        out_specs=vmem,
        compiler_params=params,
        name="unpack",
    )(target, returned.reshape(capacity, slot_count, head_width))
    count = held_count * groups
    sender = jnp.arange(capacity * groups) % capacity // per_owner
    place = pooled_slots[:, early * HD + HD - 1].astype(jnp.int32)
    live = pooled_slots[:, early * HD] > 0
    response = jnp.where(live, sender * held_count + place, count)
    order = (jnp.arange(count)[:, None] == response[None, :]).astype(jnp.bfloat16)
    pooled_all = jnp.concatenate(
        [
            jnp.dot(order, slots, preferred_element_type=jnp.float32).astype(jnp.bfloat16)
            for slots in (pooled_slots[:, : early * HD], pooled_late)
        ],
        axis=1,
    )
    share = count // planes
    partial_mix = jnp.dot(pooled_all, output_weight, preferred_element_type=jnp.float32)
    columns = output_weight.shape[1]
    scaled_head = norm_gain * reward_head
    shares = lax.all_to_all(
        partial_mix.astype(jnp.bfloat16).reshape(planes, share, columns),
        "mp",
        split_axis=0,
        concat_axis=0,
        tiled=True,
    )
    part = jnp.sum(shares.astype(jnp.float32), axis=0) + lax.dynamic_slice_in_dim(
        residual, model_rank * share, share, 0
    ).astype(jnp.float32)
    combined = lax.all_gather(part.astype(jnp.bfloat16), "mp", axis=0, tiled=True).astype(
        jnp.float32
    )
    square_sum = jnp.sum(combined * combined, axis=1)
    signal = jnp.sum(combined * scaled_head[None, :], axis=1)
    square_sum, signal = lax.psum((square_sum, signal), "dp")
    inverse = lax.rsqrt(square_sum / D + EPSILON)
    rewards = inverse * signal
    pair_loss, reward_slope = bradley_terry(rewards, pairing)
    direct_term = reward_slope * inverse
    norm_term = reward_slope * inverse * inverse * inverse * signal / D
    upstream = direct_term[:, None] * scaled_head[None, :] - norm_term[:, None] * combined
    head_gradient = jnp.sum(direct_term[:, None] * combined * norm_gain[None, :], axis=0)
    upstream_half = upstream.astype(jnp.bfloat16)
    slope_part = lax.dot_general(
        upstream_half,
        output_weight,
        (((1,), (1,)), ((), ())),
        preferred_element_type=jnp.float32,
    ).astype(jnp.bfloat16)
    slope_parts = lax.all_to_all(
        slope_part.reshape(groups, held_count, head_width),
        "dp",
        split_axis=0,
        concat_axis=0,
        tiled=True,
    )
    weight_gradient = lax.dot_general(
        pooled_all, upstream_half, (((0,), (0,)), ((), ())), preferred_element_type=jnp.float32
    )
    pooled_gradient = jnp.sum(slope_parts.astype(jnp.float32), axis=0)
    return (attention_rows, rewards, pair_loss, weight_gradient, head_gradient, pooled_gradient)


MESH = pl.DeviceIdType.MESH
NT = (((1,), (1,)), ((), ()))
TN = (((0,), (0,)), ((), ()))


def plan_kernel(per, chunk_slots, window, owners, lengths, query, keys, packed, info, target, count, got, held, sems):
    me = lax.axis_index("dp")
    groups = count.shape[0]
    held_count = query.shape[0]
    width = query.shape[2]
    span = window * HD
    first = jnp.minimum(
        lax.axis_index("mp") * (width // HD) // (Q_HEADS // KV_HEADS), KV_HEADS - window
    )
    columns = pl.ds(pl.multiple_of(first * HD, HD), span)
    loads = [
        pltpu.make_async_copy(query, got, sems.at[0]),
        pltpu.make_async_copy(keys.at[0, :, :, columns], held.at[0], sems.at[1]),
        pltpu.make_async_copy(keys.at[1, :, :, columns], held.at[1], sems.at[2]),
    ]
    for load in loads:
        load.start()
    for owner in range(groups):
        count[owner] = 0
    spot = lax.broadcasted_iota(jnp.int32, (8, HD), 0) * HD + lax.broadcasted_iota(
        jnp.int32, (8, HD), 1
    )
    block = groups * chunk_slots

    def place(r, rows):
        owner = owners[r]
        j = count[owner]
        count[owner] = j + 1
        target[r] = owner * per + j
        info[owner, pl.ds(j, 1), :] = jnp.full((1, HD), lengths[r], jnp.int32).astype(jnp.float32)
        row = (
            j // chunk_slots * (groups * block) + owner * block + j % chunk_slots * groups + me
        )
        return jnp.where(spot == me * held_count + r, row, rows)

    rows = lax.fori_loop(0, held_count, place, jnp.zeros((8, HD), jnp.int32))
    for owner in range(groups):
        info[owner, pl.ds(8, 8), :] = rows.astype(jnp.float32)
    for load in loads:
        load.wait()

    def move(r, carry):
        p = target[r]
        packed[p, :, pl.ds(0, width)] = got[r]
        packed[p, :, pl.ds(width, span)] = held[0, r]
        packed[p, :, pl.ds(width + span, span)] = held[1, r]
        return carry

    lax.fori_loop(0, held_count, move, 0)


def layer_kernel(
    sizes,
    packed,
    info,
    cache,
    weight,
    residual,
    gain,
    head,
    pairing,
    returned,
    pooled,
    upstream,
    reduced,
    head_gradient,
    rewards_out,
    loss_out,
    land,
    info_land,
    kv,
    w,
    res,
    place,
    sign,
    shifted,
    attended,
    own,
    z_send,
    z_land,
    z_total,
    combined,
    stat,
    stat_land,
    full_parts,
    half_parts,
    near_land,
    far_send,
    far_land,
    load_sem,
    info_sem,
    move_sem,
    local_sem,
    pool_sem,
    pass_sem,
    back_sem,
    z_sem,
    t_sem,
    stat_sem,
    near_sem,
    far_sem,
):
    groups, planes, per, chunk_slots, window, sub = sizes
    me = lax.axis_index("dp")
    rank = lax.axis_index("mp")
    chips = groups // 2
    chip = me // 2
    core = me % 2
    sibling = chip * 2 + 1 - core
    chunks = per // chunk_slots
    block = groups * chunk_slots
    unit = chunk_slots * 8
    rows = block * 8
    mixed = groups * block
    width = attended.shape[1]
    local_heads = width // HD
    group_size = Q_HEADS // KV_HEADS
    stack = math.gcd(local_heads, group_size)
    span = window * HD
    count = pooled.shape[0]
    first = jnp.minimum(rank * local_heads // group_size, KV_HEADS - window)
    columns = pl.ds(pl.multiple_of(first * HD, HD), span)

    def remote(src, dst, sem, index, **where):
        return pltpu.make_async_remote_copy(
            src_ref=src,
            dst_ref=dst,
            send_sem=sem.at[(0,) + index],
            recv_sem=sem.at[(1,) + index],
            device_id=where,
            device_id_type=MESH,
        )

    def at(start, size):
        return pl.ds(pl.multiple_of(start, size), size)

    loads = [
        pltpu.make_async_copy(cache.at[0, 0, :, columns], kv.at[0], load_sem.at[0]),
        pltpu.make_async_copy(cache.at[1, 0, :, columns], kv.at[1], load_sem.at[1]),
        pltpu.make_async_copy(residual, res, load_sem.at[2]),
        pltpu.make_async_copy(weight, w, load_sem.at[3]),
    ]
    for load in loads:
        load.start()

    barrier = pltpu.get_barrier_semaphore()
    for d in range(1, groups):
        pl.semaphore_signal(
            barrier, inc=1, device_id={"dp": (me + d) % groups}, device_id_type=MESH
        )
    for d in range(1, planes):
        pl.semaphore_signal(
            barrier, inc=1, device_id={"mp": (rank + d) % planes}, device_id_type=MESH
        )
    pl.semaphore_wait(barrier, groups + planes - 2)

    infos = []
    for d in range(1, groups):
        peer = (me + d) % groups
        copy = remote(info.at[peer], info_land.at[me], info_sem, (d - 1,), dp=peer)
        copy.start()
        infos.append(copy)
    moves = []
    locals_ = []
    for c in range(chunks):
        moves.append([])
        for d in range(1, groups):
            peer = (me + d) % groups
            copy = remote(
                packed.at[at((peer * chunks + c) * unit, unit), :],
                land.at[at((c * groups + me) * unit, unit), :],
                move_sem,
                (c * (groups - 1) + d - 1,),
                dp=peer,
            )
            copy.start()
            moves[c].append(copy)
        copy = pltpu.make_async_copy(
            packed.at[at((me * chunks + c) * unit, unit), :],
            land.at[at((c * groups + me) * unit, unit), :],
            local_sem.at[c],
        )
        copy.start()
        locals_.append(copy)

    info_land[me] = info[me]
    for copy in infos:
        copy.wait_recv()
    row_of = info_land[0, pl.ds(8, 8), :]
    for g in range(1, groups):
        row_of = row_of + info_land[g, pl.ds(8, 8), :]
    row_of = row_of.astype(jnp.int32)
    row_at = lax.broadcasted_iota(jnp.int32, (count, HD), 0)
    for a in range(count // HD):
        place[:, a * HD : (a + 1) * HD] = jnp.where(
            row_at == row_of[a : a + 1, :], 1.0, 0.0
        ).astype(jnp.bfloat16)
    asked = jnp.where(
        lax.broadcasted_iota(jnp.int32, (count, count), 0) == pairing[...], 1.0, 0.0
    ).astype(jnp.bfloat16)
    pair = lax.broadcasted_iota(jnp.int32, (count // 2, count), 0) * 2
    entry = lax.broadcasted_iota(jnp.int32, (count // 2, count), 1)
    side = jnp.where(entry == pair, 1.0, jnp.where(entry == pair + 1, -1.0, 0.0))
    chosen = lax.dot_general(
        side.astype(jnp.bfloat16), asked, NT, preferred_element_type=jnp.float32
    )
    sign[...] = lax.dot_general(
        chosen.astype(jnp.bfloat16), place[...], NT, preferred_element_type=jnp.float32
    )
    loads[2].wait()
    shifted[...] = jnp.dot(place[...], res[...], preferred_element_type=jnp.float32)

    scale = math.log2(math.e) / math.sqrt(HD)
    tall = stack * rows

    def attend(c):
        here = pl.ds(c * rows, rows)
        row = lax.broadcasted_iota(jnp.int32, (tall, rows), 0) % rows
        col = lax.broadcasted_iota(jnp.int32, (tall, rows), 1)
        causal = (row // 8 == col // 8) & (col <= row)
        for s in range(local_heads // stack):
            part = (rank * local_heads + stack * s) // group_size - first
            query = jnp.concatenate(
                [
                    land[here, h * HD : (h + 1) * HD]
                    for h in range(s * stack, (s + 1) * stack)
                ],
                axis=0,
            )
            own_k = land[here, pl.ds(pl.multiple_of(width + part * HD, HD), HD)]
            own_v = land[here, pl.ds(pl.multiple_of(width + span + part * HD, HD), HD)]
            key = kv[0, :, pl.ds(pl.multiple_of(part * HD, HD), HD)]
            value = kv[1, :, pl.ds(pl.multiple_of(part * HD, HD), HD)]
            far = lax.dot_general(query, key, NT, preferred_element_type=jnp.float32)
            near = lax.dot_general(query, own_k, NT, preferred_element_type=jnp.float32)
            near = jnp.where(causal, near, -1e30)
            top = jnp.maximum(
                jnp.max(far, axis=1, keepdims=True), jnp.max(near, axis=1, keepdims=True)
            )
            far = jnp.exp2((far - top) * scale).astype(jnp.bfloat16)
            near = jnp.exp2((near - top) * scale).astype(jnp.bfloat16)
            ones = lambda v: jnp.concatenate([v, jnp.ones_like(v)], axis=1)
            both = jnp.dot(far, ones(value), preferred_element_type=jnp.float32)
            both += jnp.dot(near, ones(own_v), preferred_element_type=jnp.float32)
            out = (both[:, :HD] / both[:, HD:]).astype(jnp.bfloat16)
            for h in range(stack):
                attended[here, (s * stack + h) * HD : (s * stack + h + 1) * HD] = out[
                    h * rows : (h + 1) * rows
                ]

    pools = []
    passes = []

    def share(c):
        slots = [
            jnp.concatenate(
                [info_land[g, pl.ds(c * chunk_slots + k, 1), :] for g in range(groups)], axis=0
            )
            for k in range(chunk_slots)
        ]
        length = jnp.concatenate(slots, axis=0).astype(jnp.int32)
        i = lax.broadcasted_iota(jnp.int32, (block, HD), 0)
        col = lax.broadcasted_iota(jnp.int32, (block, HD), 1)
        start = (i % groups * chunk_slots + i // groups) * 8 - 1
        pick = jnp.where(col == start + length, 1.0, 0.0).astype(jnp.bfloat16)
        last = jnp.dot(
            pick, attended[pl.ds(c * rows, rows), :], preferred_element_type=jnp.float32
        )
        mine = at(c * mixed + me * block, block)
        pooled[mine, :] = last.astype(jnp.bfloat16)
        sent = []
        for q in range(1, chips):
            sent.append(
                remote(
                    pooled.at[mine, :],
                    pooled.at[mine, :],
                    pool_sem,
                    (c * chips + q,),
                    dp=(chip + q) % chips * 2 + core,
                )
            )
        sent.append(
            remote(
                pooled.at[mine, :], pooled.at[mine, :], pool_sem, (c * chips,), dp=sibling
            )
        )
        for copy in sent:
            copy.start()
        pools.append(sent)

    def pass_on(c):
        sent = []
        for q in range(1, chips):
            pools[c][q - 1].wait_recv()
            source = (chip + chips - q) % chips * 2 + core
            there = at(c * mixed + source * block, block)
            copy = remote(
                pooled.at[there, :],
                pooled.at[there, :],
                pass_sem,
                (c * (chips - 1) + q - 1,),
                dp=sibling,
            )
            copy.start()
            sent.append(copy)
        passes.append(sent)

    depth = jnp.minimum(rank, planes - 1 - rank)
    centre = planes // 2 - 1
    is_centre = depth == centre
    low = rank < planes // 2
    inward = jnp.where(low, rank + 1, rank - 1)
    outward = jnp.where(low, rank - 1, rank + 1)
    outward = jnp.where(depth == 0, inward, outward)
    slot = jnp.where(is_centre, 1, 0)
    steps = mixed // sub
    z_copies = [
        remote(
            z_send.at[pl.ds(n * sub, sub), :],
            z_land.at[slot, pl.ds(n * sub, sub), :],
            z_sem,
            (slot, n),
            mp=inward,
        )
        for n in range(chunks * steps)
    ]
    z_waits = [
        [
            remote(
                z_send.at[pl.ds(n * sub, sub), :],
                z_land.at[k, pl.ds(n * sub, sub), :],
                z_sem,
                (k, n),
                mp=inward,
            )
            for n in range(chunks * steps)
        ]
        for k in range(2)
    ]
    t_copies = [
        remote(
            z_total.at[pl.ds(n * sub, sub), :],
            z_total.at[pl.ds(n * sub, sub), :],
            t_sem,
            (n,),
            mp=outward,
        )
        for n in range(chunks * steps)
    ]

    def mix(c):
        for copy in passes[c]:
            copy.wait_recv()
        pools[c][-1].wait_recv()
        if c == 0:
            loads[3].wait()
        here = pl.ds(c * mixed, mixed)
        product = jnp.dot(pooled[here, :], w[...], preferred_element_type=jnp.float32)
        own[here, :] = product
        z_send[here, :] = product.astype(jnp.bfloat16)

        @pl.when(depth == 0)
        def _():
            for n in range(c * steps, (c + 1) * steps):
                z_copies[n].start()

    def inner(n):
        here = pl.ds(n * sub, sub)

        @pl.when(depth > 0)
        def _():
            z_waits[0][n].wait_recv()
            z_send[here, :] = (own[here, :] + z_land[0, here, :].astype(jnp.float32)).astype(
                jnp.bfloat16
            )
            z_copies[n].start()

    scaled_head = gain[...] * head[...]

    def finish(n):
        here = pl.ds(n * sub, sub)

        @pl.when(is_centre)
        def _():
            z_waits[1][n].wait_recv()
            z_total[here, :] = (
                z_send[here, :].astype(jnp.float32) + z_land[1, here, :].astype(jnp.float32)
            ).astype(jnp.bfloat16)

        @pl.when(depth < centre)
        def _():
            t_copies[n].wait_recv()

        @pl.when(depth > 0)
        def _():
            t_copies[n].start()

        whole = z_total[here, :].astype(jnp.float32) + shifted[here, :]
        combined[here, :] = whole
        square = jnp.sum(whole * whole, axis=1, keepdims=True)
        signal = jnp.sum(whole * scaled_head, axis=1, keepdims=True)
        lane = lax.broadcasted_iota(jnp.int32, (sub, HD), 1)
        this = lax.broadcasted_iota(jnp.int32, (sub, HD), 0) + n * sub % HD
        line = n * sub // HD
        for k, column in enumerate((square, signal)):
            spread = jnp.sum(jnp.where(lane == this, column, 0.0), axis=0, keepdims=True)
            there = pl.ds(k * (count // HD) + line, 1)
            if n * sub % HD == 0:
                stat[there, :] = spread
            else:
                stat[there, :] += spread

    backs = []

    def give_back(c):
        for d in range(1, groups):
            peer = (me + d) % groups
            copy = remote(
                attended.at[at((c * groups + peer) * unit, unit), :],
                returned.at[at((me * chunks + c) * unit, unit), :],
                back_sem,
                (c * (groups - 1) + d - 1,),
                dp=peer,
            )
            copy.start()
            backs.append(copy)
        copy = pltpu.make_async_copy(
            attended.at[at((c * groups + me) * unit, unit), :],
            returned.at[at((me * chunks + c) * unit, unit), :],
            local_sem.at[chunks + c],
        )
        copy.start()
        locals_.append(copy)

    for c in range(chunks):
        for copy in moves[c]:
            copy.wait_recv()
        locals_[c].wait()
        if c == 0:
            loads[0].wait()
            loads[1].wait()
        attend(c)
        share(c)
        if c > 0:
            pass_on(c - 1)
            mix(c - 1)
    taken = (chunks - 2) * steps
    for n in range(taken):
        inner(n)
    pass_on(chunks - 1)
    for c in range(chunks):
        give_back(c)
    mix(chunks - 1)
    total = chunks * steps
    done = 0
    for n in range(taken, total):
        inner(n)
        while done < n - 1 + (n == total - 1):
            finish(done)
            done += 1
    while done < total:
        finish(done)
        done += 1

    lines = count // HD
    stat[pl.ds(2 * lines, 8 - 2 * lines), :] = jnp.zeros((8 - 2 * lines, HD), jnp.float32)
    stats = []
    for d in range(1, groups):
        copy = remote(stat, stat_land.at[me], stat_sem, (d - 1,), dp=(me + d) % groups)
        copy.start()
        stats.append(copy)
    stat_land[me] = stat[...]
    for copy in stats:
        copy.wait_recv()
    sums = stat_land[0]
    for g in range(1, groups):
        sums = sums + stat_land[g]
    square_sum = jnp.concatenate([sums[a : a + 1] for a in range(lines)], axis=1)
    signal = jnp.concatenate([sums[lines + a : lines + a + 1] for a in range(lines)], axis=1)
    inverse = lax.rsqrt(square_sum / D + EPSILON)
    rewards = inverse * signal
    margin = jnp.sum(sign[...] * rewards, axis=1, keepdims=True)
    pairs = count // 2
    slope = -jax.nn.sigmoid(-margin) / pairs
    reward_slope = jnp.sum(sign[...] * slope, axis=0, keepdims=True)
    direct = reward_slope * inverse
    norm = direct * inverse * inverse * signal / D
    eye = lax.broadcasted_iota(jnp.int32, (HD, HD), 0) == lax.broadcasted_iota(
        jnp.int32, (HD, HD), 1
    )

    def upright(line):
        return jnp.concatenate(
            [
                jnp.sum(
                    jnp.where(eye, line[:, a * HD : (a + 1) * HD], 0.0), axis=1, keepdims=True
                )
                for a in range(lines)
            ],
            axis=0,
        )

    direct_rows = upright(direct)
    norm_rows = upright(norm)
    nears = []
    for c in range(chunks):
        here = pl.ds(c * mixed, mixed)
        upstream[here, :] = (
            direct_rows[c * mixed : (c + 1) * mixed] * scaled_head
            - norm_rows[c * mixed : (c + 1) * mixed] * combined[here, :]
        ).astype(jnp.bfloat16)
        slopes = lax.dot_general(
            upstream[here, :], w[...], NT, preferred_element_type=jnp.float32
        ).reshape(block, groups, width)
        there = pl.ds(c * block, block)
        for g in range(groups):
            full_parts[g % 2, g // 2, there, :] = slopes[:, g, :]
            half_parts[g % 2, g // 2, there, :] = slopes[:, g, :].astype(jnp.bfloat16)
        copy = remote(
            half_parts.at[1 - core, :, there, :],
            near_land.at[:, there, :],
            near_sem,
            (c,),
            dp=sibling,
        )
        copy.start()
        nears.append(copy)

    fars = []
    for c in range(chunks):
        there = pl.ds(c * block, block)
        nears[c].wait_recv()
        for q in range(chips):
            goal = (chip + q) % chips
            both = full_parts[core, goal, there, :] + near_land[goal, there, :].astype(jnp.float32)
            if q == 0:
                reduced[there, :] = both
            else:
                far_send[q - 1, there, :] = both.astype(jnp.bfloat16)
                copy = remote(
                    far_send.at[q - 1, there, :],
                    far_land.at[q - 1, there, :],
                    far_sem,
                    (c * (chips - 1) + q - 1,),
                    dp=goal * 2 + core,
                )
                copy.start()
                fars.append(copy)

    rewards_rows = upright(rewards)
    rewards_out[...] = jnp.sum(
        place[...].astype(jnp.float32) * rewards_rows, axis=0, keepdims=True
    )
    against = -margin
    soft = jnp.maximum(against, 0.0) + jnp.log1p(jnp.exp(-jnp.abs(against)))
    loss_out[...] = jnp.sum(soft, axis=0, keepdims=True) / pairs
    head_gradient[...] = jnp.sum(direct_rows * combined[...], axis=0, keepdims=True) * gain[...]

    for c in range(chunks):
        there = pl.ds(c * block, block)
        extra = None
        for q in range(1, chips):
            fars[c * (chips - 1) + q - 1].wait_recv()
            piece = far_land[q - 1, there, :].astype(jnp.float32)
            extra = piece if extra is None else extra + piece
        reduced[there, :] += extra

    for copy in backs:
        copy.wait_recv()
    for copy in locals_[chunks:]:
        copy.wait()
    sent = infos + backs + stats + nears + fars
    for group in moves + pools + passes:
        sent = sent + group
    for copy in sent + z_copies:
        copy.wait_send()

    @pl.when(depth > 0)
    def _():
        for copy in t_copies:
            copy.wait_send()


def gradient_kernel(per, chunk_slots, target, lengths, returned, reduced, pooled, upstream, rows_out, pooled_gradient, weight_gradient):
    groups = returned.shape[0] // per
    block = groups * chunk_slots

    @pl.when(pl.program_id(0) == 0)
    def _():
        token = lax.broadcasted_iota(jnp.int32, returned.shape[1:], 0)

        def body(r, carry):
            p = target[r]
            rows_out[r] = jnp.where(token < lengths[r], returned[p], jnp.zeros_like(returned[p]))
            owner = p // per
            j = p % per
            row = j // chunk_slots * block + owner * chunk_slots + j % chunk_slots
            pooled_gradient[pl.ds(r, 1), :] = reduced[pl.ds(row, 1), :]
            return carry

        lax.fori_loop(0, rows_out.shape[0], body, 0)

    weight_gradient[...] = lax.dot_general(
        pooled[...], upstream[...], TN, preferred_element_type=jnp.float32
    )


def fused_shards(
    response_query,
    response_keys,
    prompt_cache,
    lengths,
    owners,
    pairing,
    residual,
    output_weight,
    norm_gain,
    reward_head,
):
    groups = lax.axis_size("dp")
    planes = lax.axis_size("mp")
    held_count, slot_count, width = response_query.shape
    local_heads = width // HD
    group_size = Q_HEADS // KV_HEADS
    per = held_count // groups
    count = held_count * groups
    columns = output_weight.shape[1]
    prefix = prompt_cache.shape[2]
    window = kv_window(planes, local_heads)
    chunk_slots = slots_of_chunk(groups, per)
    chunks = per // chunk_slots
    block = groups * chunk_slots
    chips = groups // 2
    span = window * HD
    packed_width = width + 2 * span
    bf16, f32 = jnp.bfloat16, jnp.float32
    vmem = pl.BlockSpec(memory_space=pltpu.VMEM)
    smem = pl.BlockSpec(memory_space=pltpu.SMEM)
    hbm = pl.BlockSpec(memory_space=pl.ANY)
    packed, info, target = pl.pallas_call(
        functools.partial(plan_kernel, per, chunk_slots, window),
        out_shape=(
            jax.ShapeDtypeStruct((held_count, slot_count, packed_width), bf16),
            jax.ShapeDtypeStruct((groups, 16, HD), f32),
            jax.ShapeDtypeStruct((held_count,), jnp.int32),
        ),
        in_specs=[smem, smem, hbm, hbm],
        out_specs=(vmem, vmem, smem),
        scratch_shapes=[
            pltpu.SMEM((groups,), jnp.int32),
            pltpu.VMEM((held_count, slot_count, width), bf16),
            pltpu.VMEM((2, held_count, slot_count, span), bf16),
            pltpu.SemaphoreType.DMA((3,)),
        ],
        compiler_params=pltpu.CompilerParams(vmem_limit_bytes=16 << 20),
        name="plan",
    )(owners, lengths, response_query, response_keys)
    slots = held_count * slot_count
    sub = SUB
    steps = count // sub
    dma = lambda *shape: pltpu.SemaphoreType.DMA(shape)
    returned, pooled, upstream, reduced, head_gradient, rewards, loss = pl.pallas_call(
        functools.partial(
            layer_kernel, (groups, planes, per, chunk_slots, window, sub)
        ),
        out_shape=(
            jax.ShapeDtypeStruct((slots, width), bf16),
            jax.ShapeDtypeStruct((count, width), bf16),
            jax.ShapeDtypeStruct((count, columns), bf16),
            jax.ShapeDtypeStruct((held_count, width), f32),
            jax.ShapeDtypeStruct((1, columns), f32),
            jax.ShapeDtypeStruct((1, count), f32),
            jax.ShapeDtypeStruct((1, 1), f32),
        ),
        in_specs=[vmem, vmem, hbm, hbm, hbm, vmem, vmem, vmem],
        out_specs=(vmem,) * 7,
        scratch_shapes=[
            pltpu.VMEM((slots, packed_width), bf16),
            pltpu.VMEM((groups, 16, HD), f32),
            pltpu.VMEM((2, prefix, span), bf16),
            pltpu.VMEM((width, columns), bf16),
            pltpu.VMEM((count, columns), bf16),
            pltpu.VMEM((count, count), bf16),
            pltpu.VMEM((count // 2, count), f32),
            pltpu.VMEM((count, columns), f32),
            pltpu.VMEM((slots, width), bf16),
            pltpu.VMEM((count, columns), f32),
            pltpu.VMEM((count, columns), bf16),
            pltpu.VMEM((2, count, columns), bf16),
            pltpu.VMEM((count, columns), bf16),
            pltpu.VMEM((count, columns), f32),
            pltpu.VMEM((8, HD), f32),
            pltpu.VMEM((groups, 8, HD), f32),
            pltpu.VMEM((2, chips, held_count, width), f32),
            pltpu.VMEM((2, chips, held_count, width), bf16),
            pltpu.VMEM((chips, held_count, width), bf16),
            pltpu.VMEM((chips - 1, held_count, width), bf16),
            pltpu.VMEM((chips - 1, held_count, width), bf16),
            dma(4),
            dma(2, groups - 1),
            dma(2, chunks * (groups - 1)),
            dma(2 * chunks),
            dma(2, chunks * chips),
            dma(2, chunks * (chips - 1)),
            dma(2, chunks * (groups - 1)),
            dma(2, 2, steps),
            dma(2, steps),
            dma(2, groups - 1),
            dma(2, chunks),
            dma(2, chunks * (chips - 1)),
        ],
        compiler_params=pltpu.CompilerParams(
            collective_id=0, has_side_effects=True, vmem_limit_bytes=44 << 20
        ),
        name="layer",
    )(
        packed.reshape(slots, packed_width),
        info,
        prompt_cache,
        output_weight,
        residual,
        norm_gain[None],
        reward_head[None],
        pairing[None],
    )
    tile = 256
    attention_rows, pooled_gradient, weight_gradient = pl.pallas_call(
        functools.partial(gradient_kernel, per, chunk_slots),
        out_shape=(
            jax.ShapeDtypeStruct(response_query.shape, bf16),
            jax.ShapeDtypeStruct((held_count, width), f32),
            jax.ShapeDtypeStruct((width, columns), f32),
        ),
        grid=(width // tile,),
        in_specs=[
            smem,
            smem,
            pl.BlockSpec((held_count, slot_count, width), lambda i: (0, 0, 0)),
            pl.BlockSpec((held_count, width), lambda i: (0, 0)),
            pl.BlockSpec((count, tile), lambda i: (0, i)),
            pl.BlockSpec((count, columns), lambda i: (0, 0)),
        ],
        out_specs=(
            pl.BlockSpec((held_count, slot_count, width), lambda i: (0, 0, 0)),
            pl.BlockSpec((held_count, width), lambda i: (0, 0)),
            pl.BlockSpec((tile, columns), lambda i: (i, 0)),
        ),
        compiler_params=pltpu.CompilerParams(vmem_limit_bytes=32 << 20),
        name="gradient",
    )(
        target,
        lengths,
        returned.reshape(held_count, slot_count, width),
        reduced,
        pooled,
        upstream,
    )
    return (
        attention_rows,
        rewards[0],
        loss[0, 0],
        weight_gradient,
        head_gradient[0],
        pooled_gradient,
    )


SUB = 64


def kv_window(planes, local_heads):
    group_size = Q_HEADS // KV_HEADS
    return max(
        (m * local_heads + local_heads - 1) // group_size - m * local_heads // group_size + 1
        for m in range(planes)
    )


def slots_of_chunk(groups, per):
    for slots in range(1, per + 1):
        if per % slots == 0 and slots * groups % 16 == 0:
            return slots
    return 0


def fits(shape, responses):
    groups, planes = shape["dp"], shape["mp"]
    held = responses // groups
    if held % groups or groups % 2 or planes % 2:
        return False
    slots = slots_of_chunk(groups, held // groups)
    return bool(slots) and slots * groups * 8 == HD and responses % HD == 0 and responses <= 3 * HD


def shards(*args):
    held = args[0].shape[0]
    groups = lax.axis_size("dp")
    sizes = {"dp": groups, "mp": lax.axis_size("mp")}
    if fits(sizes, held * groups):
        return fused_shards(*args)
    return stepwise_shards(*args)


def solution(mesh):
    placed = (
        P("dp", None, "mp"),
        P(None, "dp", None, None),
        P(None, "dp", None, None),
        P("dp"),
        P("dp"),
        P(),
        P(None, "dp"),
        P("mp", "dp"),
        P("dp"),
        P("dp"),
    )
    return jax.shard_map(
        shards,
        mesh=mesh,
        in_specs=placed,
        out_specs=(P("dp", None, "mp"), P(), P(), P("mp", "dp"), P("dp"), P("dp", "mp")),
        check_vma=False,
    )
```

```python
import functools
import math

import jax
import jax.numpy as jnp
from jax import lax
from jax.experimental import pallas as pl
from jax.experimental.pallas import tpu as pltpu
from jax.sharding import PartitionSpec as P

D = 8192
HD = 128
Q_HEADS = 48
KV_HEADS = 6


EPSILON = 1e-05


def bradley_terry(rewards, pairing):
    count = rewards.shape[0]
    chosen = pairing[0::2, None] == jnp.arange(count)[None, :]
    rejected = pairing[1::2, None] == jnp.arange(count)[None, :]
    sign = chosen.astype(jnp.float32) - rejected.astype(jnp.float32)
    margin = jnp.sum(sign * rewards[None, :], axis=1)
    loss_value = jnp.mean(jax.nn.softplus(-margin))
    slope = -jax.nn.sigmoid(-margin) / margin.shape[0]
    reward_slope = jnp.sum(sign * slope[:, None], axis=0)
    return (loss_value, reward_slope)


def pack_kernel(window, meta, query, keys, out, late):
    slots = out.shape[0]
    rest = late.shape[2]
    width = query.shape[2] - rest
    span = window * HD
    first = pl.multiple_of(meta[2 * slots] * HD, HD)

    def body(p, carry):
        r = meta[p]
        out[p, :, pl.ds(0, width)] = query[r, :, pl.ds(0, width)]
        late[p] = query[r, :, pl.ds(width, rest)]
        out[p, :, pl.ds(width, span)] = keys[0, r, :, pl.ds(first, span)]
        out[p, :, pl.ds(width + span, span)] = keys[1, r, :, pl.ds(first, span)]
        length = meta[slots + p].astype(jnp.float32)
        place = r.astype(jnp.float32)
        lane = lax.broadcasted_iota(jnp.int32, (out.shape[1], HD), 1)
        out[p, :, pl.ds(width + 2 * span, HD)] = jnp.where(lane < HD // 2, length, place).astype(
            jnp.bfloat16
        )
        return carry

    lax.fori_loop(0, slots, body, 0)


def attention_kernel(slot_count, placed, meta, query, own_k, own_v, lens, cache, out, pooled):
    rows = query.shape[0]
    head = pl.program_id(0)
    chunk = 128
    blocks = chunk // slot_count
    scale = math.log2(math.e) / math.sqrt(HD)
    contract = (((1,), (1,)), ((), ()))
    row = lax.broadcasted_iota(jnp.int32, (chunk, chunk), 0)
    col = lax.broadcasted_iota(jnp.int32, (chunk, chunk), 1)
    t = row % slot_count
    s = col % slot_count
    causal = (row // slot_count == col // slot_count) & (s <= t)
    s_float = s.astype(jnp.float32)
    t_float = t.astype(jnp.float32)
    gather = lax.broadcasted_iota(jnp.int32, (blocks, chunk), 0)
    member = lax.broadcasted_iota(jnp.int32, (blocks, chunk), 1)
    gather = jnp.where(gather == member // slot_count, 1.0, 0.0).astype(jnp.bfloat16)
    for start in range(0, rows, chunk):
        here = pl.ds(start, chunk)
        q = query[here, :]
        length = jnp.broadcast_to(lens[here, :].astype(jnp.float32)[:, 0:1], (chunk, chunk))
        far = lax.dot_general(q, cache[0, 0], contract, preferred_element_type=jnp.float32)
        near = lax.dot_general(q, own_k[here, :], contract, preferred_element_type=jnp.float32)
        near = jnp.where(causal & (s_float < length), near, -jnp.inf)
        top = jnp.maximum(
            jnp.max(far, axis=1, keepdims=True), jnp.max(near, axis=1, keepdims=True)
        )
        far = jnp.exp2((far - top) * scale)
        near = jnp.exp2((near - top) * scale)
        total = jnp.sum(far, axis=1, keepdims=True) + jnp.sum(near, axis=1, keepdims=True)
        value = jnp.dot(far.astype(jnp.bfloat16), cache[1, 0], preferred_element_type=jnp.float32)
        value += jnp.dot(
            near.astype(jnp.bfloat16), own_v[here, :], preferred_element_type=jnp.float32
        )
        value = jnp.where(t_float < length, value / total, 0.0)
        out[here, :] = value.astype(jnp.bfloat16)
        last = jnp.where(t_float == length - 1.0, value, 0.0)
        last = jnp.dot(gather, last.astype(jnp.bfloat16), preferred_element_type=jnp.float32)
        there = pl.ds(start // slot_count, blocks)
        pooled[there, pl.ds(pl.multiple_of(head * HD, HD), HD)] = last.astype(jnp.bfloat16)

        if placed:

            @pl.when(head == 0)
            def _():
                place = lens[here, :].astype(jnp.float32).reshape(blocks, slot_count, HD)
                pooled[there, pl.ds(pooled.shape[1] - HD, HD)] = jnp.max(place, axis=1).astype(
                    jnp.bfloat16
                )


def unpack_kernel(meta, returned, out):
    def body(r, carry):
        out[r] = returned[meta[r]]
        return carry

    lax.fori_loop(0, out.shape[0], body, 0)


def stepwise_shards(
    response_query,
    response_keys,
    prompt_cache,
    lengths,
    owners,
    pairing,
    residual,
    output_weight,
    norm_gain,
    reward_head,
):
    groups = lax.axis_size("dp")
    planes = lax.axis_size("mp")
    model_rank = lax.axis_index("mp")
    held_count, slot_count, head_width = response_query.shape
    local_heads = head_width // HD
    group_size = Q_HEADS // KV_HEADS
    per_owner = (held_count + groups - 1) // groups
    capacity = groups * per_owner
    window = max(
        (m * local_heads + local_heads - 1) // group_size - m * local_heads // group_size + 1
        for m in range(planes)
    )
    first_head = jnp.minimum(model_rank * local_heads // group_size, KV_HEADS - window)
    head_kv = (model_rank * local_heads + jnp.arange(local_heads)) // group_size
    positions = jnp.arange(held_count)
    earlier = (owners[None, :] == owners[:, None]) & (positions[None, :] < positions[:, None])
    target = (owners * per_owner + jnp.sum(earlier, axis=1)).astype(jnp.int32)
    sent_from = (target[None, :] == jnp.arange(capacity)[:, None]).astype(jnp.int32)
    source = jnp.sum(sent_from * positions[None, :], axis=1)
    slot_length = jnp.sum(sent_from * lengths[None, :], axis=1)
    params = pltpu.CompilerParams(vmem_limit_bytes=40 * 1024 * 1024)
    vmem = pl.BlockSpec(memory_space=pltpu.VMEM)
    smem = pl.BlockSpec(memory_space=pltpu.SMEM)
    early = local_heads - local_heads // 2
    late_width = local_heads // 2 * HD
    packed_width = early * HD + (2 * window + 1) * HD
    packed, late = pl.pallas_call(
        functools.partial(pack_kernel, window),
        out_shape=(
            jax.ShapeDtypeStruct((capacity, slot_count, packed_width), jnp.bfloat16),
            jax.ShapeDtypeStruct((capacity, slot_count, late_width), jnp.bfloat16),
        ),
        in_specs=[smem, vmem, vmem],
        out_specs=(vmem, vmem),
        compiler_params=params,
        name="pack",
    )(
        jnp.concatenate([source, slot_length, first_head[None]]).astype(jnp.int32),
        response_query,
        response_keys,
    )
    packed = packed.reshape(groups, per_owner, slot_count, packed_width)
    arrived = lax.all_to_all(packed, "dp", split_axis=0, concat_axis=0, tiled=True)
    late = late.reshape(groups, per_owner, slot_count, late_width)
    late = lax.all_to_all(late, "dp", split_axis=0, concat_axis=0, tiled=True)
    rows = capacity * slot_count
    late = late.reshape(rows, late_width)
    arrived = arrived.reshape(rows, packed_width)
    block = (rows, HD)

    def attend(query, head_base, heads, placed):
        pooled_width = (heads + placed) * HD
        at = lambda meta, h: meta[local_heads + head_base + h]
        return pl.pallas_call(
            functools.partial(attention_kernel, slot_count, placed),
            out_shape=(
                jax.ShapeDtypeStruct((rows, heads * HD), jnp.bfloat16),
                jax.ShapeDtypeStruct((capacity, pooled_width), jnp.bfloat16),
            ),
            grid_spec=pltpu.PrefetchScalarGridSpec(
                num_scalar_prefetch=1,
                grid=(heads,),
                in_specs=[
                    pl.BlockSpec(block, lambda h, meta: (0, h)),
                    pl.BlockSpec(block, lambda h, meta: (0, early + at(meta, h))),
                    pl.BlockSpec(block, lambda h, meta: (0, early + window + at(meta, h))),
                    pl.BlockSpec(block, lambda h, meta: (0, early + 2 * window)),
                    pl.BlockSpec(
                        (2, 1, prompt_cache.shape[2], HD),
                        lambda h, meta: (0, 0, 0, meta[head_base + h]),
                    ),
                ],
                out_specs=(
                    pl.BlockSpec(block, lambda h, meta: (0, h)),
                    pl.BlockSpec((capacity, pooled_width), lambda h, meta: (0, 0)),
                ),
            ),
            compiler_params=params,
            cost_estimate=pl.CostEstimate(
                flops=4 * rows * heads * HD * prompt_cache.shape[2],
                bytes_accessed=8 * rows * heads * HD,
                transcendentals=rows * heads * prompt_cache.shape[2],
            ),
            name="attention_early" if placed else "attention_late",
        )(
            jnp.concatenate([head_kv, head_kv - first_head]).astype(jnp.int32),
            query,
            arrived,
            arrived,
            arrived,
            prompt_cache,
        )

    def share_rows(own):
        copies = jnp.broadcast_to(own[None], (groups,) + own.shape)
        copies = lax.all_to_all(copies, "dp", split_axis=0, concat_axis=0, tiled=True)
        return copies.reshape(groups * own.shape[0], own.shape[1])

    attended_early, pooled_early = attend(arrived, 0, early, True)
    pooled_slots = share_rows(pooled_early)
    attended_late, pooled_late = attend(late, early, local_heads - early, False)
    pooled_late = share_rows(pooled_late)
    attended = jnp.concatenate([attended_early, attended_late], axis=1)
    result = attended.reshape(groups, per_owner, slot_count, head_width)
    returned = lax.all_to_all(result, "dp", split_axis=0, concat_axis=0, tiled=True)
    attention_rows = pl.pallas_call(
        unpack_kernel,
        out_shape=jax.ShapeDtypeStruct(response_query.shape, jnp.bfloat16),
        in_specs=[smem, vmem],
        out_specs=vmem,
        compiler_params=params,
        name="unpack",
    )(target, returned.reshape(capacity, slot_count, head_width))
    count = held_count * groups
    sender = jnp.arange(capacity * groups) % capacity // per_owner
    place = pooled_slots[:, early * HD + HD - 1].astype(jnp.int32)
    live = pooled_slots[:, early * HD] > 0
    response = jnp.where(live, sender * held_count + place, count)
    order = (jnp.arange(count)[:, None] == response[None, :]).astype(jnp.bfloat16)
    pooled_all = jnp.concatenate(
        [
            jnp.dot(order, slots, preferred_element_type=jnp.float32).astype(jnp.bfloat16)
            for slots in (pooled_slots[:, : early * HD], pooled_late)
        ],
        axis=1,
    )
    share = count // planes
    partial_mix = jnp.dot(pooled_all, output_weight, preferred_element_type=jnp.float32)
    columns = output_weight.shape[1]
    scaled_head = norm_gain * reward_head
    shares = lax.all_to_all(
        partial_mix.astype(jnp.bfloat16).reshape(planes, share, columns),
        "mp",
        split_axis=0,
        concat_axis=0,
        tiled=True,
    )
    part = jnp.sum(shares.astype(jnp.float32), axis=0) + lax.dynamic_slice_in_dim(
        residual, model_rank * share, share, 0
    ).astype(jnp.float32)
    combined = lax.all_gather(part.astype(jnp.bfloat16), "mp", axis=0, tiled=True).astype(
        jnp.float32
    )
    square_sum = jnp.sum(combined * combined, axis=1)
    signal = jnp.sum(combined * scaled_head[None, :], axis=1)
    square_sum, signal = lax.psum((square_sum, signal), "dp")
    inverse = lax.rsqrt(square_sum / D + EPSILON)
    rewards = inverse * signal
    pair_loss, reward_slope = bradley_terry(rewards, pairing)
    direct_term = reward_slope * inverse
    norm_term = reward_slope * inverse * inverse * inverse * signal / D
    upstream = direct_term[:, None] * scaled_head[None, :] - norm_term[:, None] * combined
    head_gradient = jnp.sum(direct_term[:, None] * combined * norm_gain[None, :], axis=0)
    upstream_half = upstream.astype(jnp.bfloat16)
    slope_part = lax.dot_general(
        upstream_half,
        output_weight,
        (((1,), (1,)), ((), ())),
        preferred_element_type=jnp.float32,
    ).astype(jnp.bfloat16)
    slope_parts = lax.all_to_all(
        slope_part.reshape(groups, held_count, head_width),
        "dp",
        split_axis=0,
        concat_axis=0,
        tiled=True,
    )
    weight_gradient = lax.dot_general(
        pooled_all, upstream_half, (((0,), (0,)), ((), ())), preferred_element_type=jnp.float32
    )
    pooled_gradient = jnp.sum(slope_parts.astype(jnp.float32), axis=0)
    return (attention_rows, rewards, pair_loss, weight_gradient, head_gradient, pooled_gradient)


MESH = pl.DeviceIdType.MESH
NT = (((1,), (1,)), ((), ()))
TN = (((0,), (0,)), ((), ()))


def plan_kernel(per, chunk_slots, window, owners, lengths, query, keys, packed, info, target, count, got, held, sems):
    me = lax.axis_index("dp")
    groups = count.shape[0]
    held_count = query.shape[0]
    width = query.shape[2]
    span = window * HD
    first = jnp.minimum(
        lax.axis_index("mp") * (width // HD) // (Q_HEADS // KV_HEADS), KV_HEADS - window
    )
    columns = pl.ds(pl.multiple_of(first * HD, HD), span)
    loads = [
        pltpu.make_async_copy(query, got, sems.at[0]),
        pltpu.make_async_copy(keys.at[0, :, :, columns], held.at[0], sems.at[1]),
        pltpu.make_async_copy(keys.at[1, :, :, columns], held.at[1], sems.at[2]),
    ]
    for load in loads:
        load.start()
    for owner in range(groups):
        count[owner] = 0
    spot = lax.broadcasted_iota(jnp.int32, (8, HD), 0) * HD + lax.broadcasted_iota(
        jnp.int32, (8, HD), 1
    )
    block = groups * chunk_slots

    def place(r, rows):
        owner = owners[r]
        j = count[owner]
        count[owner] = j + 1
        target[r] = owner * per + j
        info[owner, pl.ds(j, 1), :] = jnp.full((1, HD), lengths[r], jnp.int32).astype(jnp.float32)
        row = (
            j // chunk_slots * (groups * block) + owner * block + j % chunk_slots * groups + me
        )
        return jnp.where(spot == me * held_count + r, row, rows)

    rows = lax.fori_loop(0, held_count, place, jnp.zeros((8, HD), jnp.int32))
    for owner in range(groups):
        info[owner, pl.ds(8, 8), :] = rows.astype(jnp.float32)
    for load in loads:
        load.wait()

    def move(r, carry):
        p = target[r]
        packed[p, :, pl.ds(0, width)] = got[r]
        packed[p, :, pl.ds(width, span)] = held[0, r]
        packed[p, :, pl.ds(width + span, span)] = held[1, r]
        return carry

    lax.fori_loop(0, held_count, move, 0)


def layer_kernel(
    sizes,
    packed,
    info,
    cache,
    weight,
    residual,
    gain,
    head,
    pairing,
    returned,
    pooled,
    upstream,
    reduced,
    head_gradient,
    rewards_out,
    loss_out,
    land,
    info_land,
    kv,
    w,
    res,
    place,
    sign,
    turn,
    shifted,
    attended,
    own,
    z_send,
    z_land,
    z_total,
    combined,
    stat,
    stat_land,
    turned,
    near_send,
    near_land,
    far_send,
    far_land,
    load_sem,
    info_sem,
    move_sem,
    local_sem,
    pool_sem,
    pass_sem,
    back_sem,
    z_sem,
    t_sem,
    stat_sem,
    near_sem,
    far_sem,
):
    groups, planes, per, chunk_slots, window, sub = sizes
    held_count = reduced.shape[0]
    me = lax.axis_index("dp")
    rank = lax.axis_index("mp")
    chips = groups // 2
    chip = me // 2
    core = me % 2
    sibling = chip * 2 + 1 - core
    chunks = per // chunk_slots
    block = groups * chunk_slots
    unit = chunk_slots * 8
    rows = block * 8
    mixed = groups * block
    width = attended.shape[1]
    local_heads = width // HD
    group_size = Q_HEADS // KV_HEADS
    stack = math.gcd(local_heads, group_size)
    span = window * HD
    count = pooled.shape[0]
    first = jnp.minimum(rank * local_heads // group_size, KV_HEADS - window)
    columns = pl.ds(pl.multiple_of(first * HD, HD), span)

    def remote(src, dst, sem, index, **where):
        return pltpu.make_async_remote_copy(
            src_ref=src,
            dst_ref=dst,
            send_sem=sem.at[(0,) + index],
            recv_sem=sem.at[(1,) + index],
            device_id=where,
            device_id_type=MESH,
        )

    def at(start, size):
        return pl.ds(pl.multiple_of(start, size), size)

    loads = [
        pltpu.make_async_copy(cache.at[0, 0, :, columns], kv.at[0], load_sem.at[0]),
        pltpu.make_async_copy(cache.at[1, 0, :, columns], kv.at[1], load_sem.at[1]),
        pltpu.make_async_copy(residual, res, load_sem.at[2]),
        pltpu.make_async_copy(weight, w, load_sem.at[3]),
    ]
    for load in loads:
        load.start()

    barrier = pltpu.get_barrier_semaphore()
    for d in range(1, groups):
        pl.semaphore_signal(
            barrier, inc=1, device_id={"dp": (me + d) % groups}, device_id_type=MESH
        )
    for d in range(1, planes):
        pl.semaphore_signal(
            barrier, inc=1, device_id={"mp": (rank + d) % planes}, device_id_type=MESH
        )
    pl.semaphore_wait(barrier, groups + planes - 2)

    infos = []
    for d in range(1, groups):
        peer = (me + d) % groups
        copy = remote(info.at[peer], info_land.at[me], info_sem, (d - 1,), dp=peer)
        copy.start()
        infos.append(copy)
    moves = []
    locals_ = []

    def dispatch(c):
        moves.append([])
        for d in range(1, groups):
            peer = (me + d) % groups
            copy = remote(
                packed.at[at((peer * chunks + c) * unit, unit), :],
                land.at[at((c * groups + me) * unit, unit), :],
                move_sem,
                (c * (groups - 1) + d - 1,),
                dp=peer,
            )
            copy.start()
            moves[c].append(copy)
        copy = pltpu.make_async_copy(
            packed.at[at((me * chunks + c) * unit, unit), :],
            land.at[at((c * groups + me) * unit, unit), :],
            local_sem.at[c],
        )
        copy.start()
        locals_.append(copy)

    dispatch(0)

    info_land[me] = info[me]
    for copy in infos:
        copy.wait_recv()
    row_of = info_land[0, pl.ds(8, 8), :]
    for g in range(1, groups):
        row_of = row_of + info_land[g, pl.ds(8, 8), :]
    row_of = row_of.astype(jnp.int32)
    row_at = lax.broadcasted_iota(jnp.int32, (count, HD), 0)
    for a in range(count // HD):
        place[:, a * HD : (a + 1) * HD] = jnp.where(
            row_at == row_of[a : a + 1, :], 1.0, 0.0
        ).astype(jnp.bfloat16)
    asked = jnp.where(
        lax.broadcasted_iota(jnp.int32, (count, count), 0) == pairing[...], 1.0, 0.0
    ).astype(jnp.bfloat16)
    pair = lax.broadcasted_iota(jnp.int32, (count // 2, count), 0) * 2
    entry = lax.broadcasted_iota(jnp.int32, (count // 2, count), 1)
    side = jnp.where(entry == pair, 1.0, jnp.where(entry == pair + 1, -1.0, 0.0))
    chosen = lax.dot_general(
        side.astype(jnp.bfloat16), asked, NT, preferred_element_type=jnp.float32
    )
    sign[...] = lax.dot_general(
        chosen.astype(jnp.bfloat16), place[...], NT, preferred_element_type=jnp.float32
    )
    loads[2].wait()
    shifted[...] = jnp.dot(place[...], res[...], preferred_element_type=jnp.float32)

    new = lax.broadcasted_iota(jnp.int32, (mixed, mixed), 0)
    old = lax.broadcasted_iota(jnp.int32, (mixed, mixed), 1)
    old_at = new % block * groups + new // block % chips * 2 + new // (block * chips)
    turn[...] = jnp.where(old == old_at, 1.0, 0.0).astype(jnp.bfloat16)

    scale = math.log2(math.e) / math.sqrt(HD)
    tall = stack * rows

    def attend(c):
        here = pl.ds(c * rows, rows)
        row = lax.broadcasted_iota(jnp.int32, (tall, rows), 0) % rows
        col = lax.broadcasted_iota(jnp.int32, (tall, rows), 1)
        causal = (row // 8 == col // 8) & (col <= row)
        for s in range(local_heads // stack):
            part = (rank * local_heads + stack * s) // group_size - first
            query = jnp.concatenate(
                [
                    land[here, h * HD : (h + 1) * HD]
                    for h in range(s * stack, (s + 1) * stack)
                ],
                axis=0,
            )
            own_k = land[here, pl.ds(pl.multiple_of(width + part * HD, HD), HD)]
            own_v = land[here, pl.ds(pl.multiple_of(width + span + part * HD, HD), HD)]
            key = kv[0, :, pl.ds(pl.multiple_of(part * HD, HD), HD)]
            value = kv[1, :, pl.ds(pl.multiple_of(part * HD, HD), HD)]
            far = lax.dot_general(query, key, NT, preferred_element_type=jnp.float32)
            near = lax.dot_general(query, own_k, NT, preferred_element_type=jnp.float32)
            near = jnp.where(causal, near, -1e30)
            top = jnp.maximum(
                jnp.max(far, axis=1, keepdims=True), jnp.max(near, axis=1, keepdims=True)
            )
            far = jnp.exp2((far - top) * scale).astype(jnp.bfloat16)
            near = jnp.exp2((near - top) * scale).astype(jnp.bfloat16)
            ones = lambda v: jnp.concatenate([v, jnp.ones_like(v)], axis=1)
            both = jnp.dot(far, ones(value), preferred_element_type=jnp.float32)
            both += jnp.dot(near, ones(own_v), preferred_element_type=jnp.float32)
            out = (both[:, :HD] / both[:, HD:]).astype(jnp.bfloat16)
            for h in range(stack):
                attended[here, (s * stack + h) * HD : (s * stack + h + 1) * HD] = out[
                    h * rows : (h + 1) * rows
                ]

    pools = []
    passes = []

    def share(c):
        slots = [
            jnp.concatenate(
                [info_land[g, pl.ds(c * chunk_slots + k, 1), :] for g in range(groups)], axis=0
            )
            for k in range(chunk_slots)
        ]
        length = jnp.concatenate(slots, axis=0).astype(jnp.int32)
        i = lax.broadcasted_iota(jnp.int32, (block, HD), 0)
        col = lax.broadcasted_iota(jnp.int32, (block, HD), 1)
        start = (i % groups * chunk_slots + i // groups) * 8 - 1
        pick = jnp.where(col == start + length, 1.0, 0.0).astype(jnp.bfloat16)
        last = jnp.dot(
            pick, attended[pl.ds(c * rows, rows), :], preferred_element_type=jnp.float32
        )
        mine = at(c * mixed + me * block, block)
        pooled[mine, :] = last.astype(jnp.bfloat16)
        sent = []
        for q in range(1, chips):
            sent.append(
                remote(
                    pooled.at[mine, :],
                    pooled.at[mine, :],
                    pool_sem,
                    (c * chips + q,),
                    dp=(chip + q) % chips * 2 + core,
                )
            )
        sent.append(
            remote(
                pooled.at[mine, :], pooled.at[mine, :], pool_sem, (c * chips,), dp=sibling
            )
        )
        for copy in sent:
            copy.start()
        pools.append(sent)

    def pass_on(c):
        sent = []
        for q in range(1, chips):
            pools[c][q - 1].wait_recv()
            source = (chip + chips - q) % chips * 2 + core
            there = at(c * mixed + source * block, block)
            copy = remote(
                pooled.at[there, :],
                pooled.at[there, :],
                pass_sem,
                (c * (chips - 1) + q - 1,),
                dp=sibling,
            )
            copy.start()
            sent.append(copy)
        passes.append(sent)

    depth = jnp.minimum(rank, planes - 1 - rank)
    centre = planes // 2 - 1
    is_centre = depth == centre
    low = rank < planes // 2
    inward = jnp.where(low, rank + 1, rank - 1)
    outward = jnp.where(low, rank - 1, rank + 1)
    outward = jnp.where(depth == 0, inward, outward)
    slot = jnp.where(is_centre, 1, 0)
    steps = mixed // sub
    z_copies = [
        remote(
            z_send.at[pl.ds(n * sub, sub), :],
            z_land.at[slot, pl.ds(n * sub, sub), :],
            z_sem,
            (slot, n),
            mp=inward,
        )
        for n in range(chunks * steps)
    ]
    z_waits = [
        [
            remote(
                z_send.at[pl.ds(n * sub, sub), :],
                z_land.at[k, pl.ds(n * sub, sub), :],
                z_sem,
                (k, n),
                mp=inward,
            )
            for n in range(chunks * steps)
        ]
        for k in range(2)
    ]
    t_copies = [
        remote(
            z_total.at[pl.ds(n * sub, sub), :],
            z_total.at[pl.ds(n * sub, sub), :],
            t_sem,
            (n,),
            mp=outward,
        )
        for n in range(chunks * steps)
    ]

    def mix(c):
        for copy in passes[c]:
            copy.wait_recv()
        pools[c][-1].wait_recv()
        if c == 0:
            loads[3].wait()
        here = pl.ds(c * mixed, mixed)
        product = jnp.dot(pooled[here, :], w[...], preferred_element_type=jnp.float32)
        own[here, :] = product
        z_send[here, :] = product.astype(jnp.bfloat16)

        @pl.when(depth == 0)
        def _():
            for n in range(c * steps, (c + 1) * steps):
                z_copies[n].start()

    def inner(n):
        here = pl.ds(n * sub, sub)

        @pl.when(depth > 0)
        def _():
            z_waits[0][n].wait_recv()
            z_send[here, :] = (own[here, :] + z_land[0, here, :].astype(jnp.float32)).astype(
                jnp.bfloat16
            )
            z_copies[n].start()

    scaled_head = gain[...] * head[...]

    def finish(n):
        here = pl.ds(n * sub, sub)

        @pl.when(is_centre)
        def _():
            z_waits[1][n].wait_recv()
            z_total[here, :] = (
                z_send[here, :].astype(jnp.float32) + z_land[1, here, :].astype(jnp.float32)
            ).astype(jnp.bfloat16)

        @pl.when(depth < centre)
        def _():
            t_copies[n].wait_recv()

        @pl.when(depth > 0)
        def _():
            t_copies[n].start()

        whole = z_total[here, :].astype(jnp.float32) + shifted[here, :]
        combined[here, :] = whole
        square = jnp.sum(whole * whole, axis=1, keepdims=True)
        signal = jnp.sum(whole * scaled_head, axis=1, keepdims=True)
        lane = lax.broadcasted_iota(jnp.int32, (sub, HD), 1)
        this = lax.broadcasted_iota(jnp.int32, (sub, HD), 0) + n * sub % HD
        line = n * sub // HD
        for k, column in enumerate((square, signal)):
            spread = jnp.sum(jnp.where(lane == this, column, 0.0), axis=0, keepdims=True)
            there = pl.ds(k * (count // HD) + line, 1)
            if n * sub % HD == 0:
                stat[there, :] = spread
            else:
                stat[there, :] += spread

    backs = []

    def give_back(c):
        for d in range(1, groups):
            peer = (me + d) % groups
            copy = remote(
                attended.at[at((c * groups + peer) * unit, unit), :],
                returned.at[at((me * chunks + c) * unit, unit), :],
                back_sem,
                (c * (groups - 1) + d - 1,),
                dp=peer,
            )
            copy.start()
            backs.append(copy)
        copy = pltpu.make_async_copy(
            attended.at[at((c * groups + me) * unit, unit), :],
            returned.at[at((me * chunks + c) * unit, unit), :],
            local_sem.at[chunks + c],
        )
        copy.start()
        locals_.append(copy)

    for c in range(chunks):
        for copy in moves[c]:
            copy.wait_recv()
        locals_[c].wait()
        if c + 1 < chunks:
            dispatch(c + 1)
        if c == 0:
            loads[0].wait()
            loads[1].wait()
        attend(c)
        share(c)
        if c > 0:
            pass_on(c - 1)
            mix(c - 1)
    taken = (chunks - 2) * steps
    for n in range(taken):
        inner(n)
    pass_on(chunks - 1)
    for c in range(chunks):
        give_back(c)
    mix(chunks - 1)
    total = chunks * steps
    done = 0
    for n in range(taken, total):
        inner(n)
        while done < n - 1 + (n == total - 1):
            finish(done)
            done += 1
    while done < total:
        finish(done)
        done += 1

    lines = count // HD
    stat[pl.ds(2 * lines, 8 - 2 * lines), :] = jnp.zeros((8 - 2 * lines, HD), jnp.float32)
    stats = []
    for d in range(1, groups):
        copy = remote(stat, stat_land.at[me], stat_sem, (d - 1,), dp=(me + d) % groups)
        copy.start()
        stats.append(copy)
    stat_land[me] = stat[...]
    for copy in stats:
        copy.wait_recv()
    sums = stat_land[0]
    for g in range(1, groups):
        sums = sums + stat_land[g]
    square_sum = jnp.concatenate([sums[a : a + 1] for a in range(lines)], axis=1)
    signal = jnp.concatenate([sums[lines + a : lines + a + 1] for a in range(lines)], axis=1)
    inverse = lax.rsqrt(square_sum / D + EPSILON)
    rewards = inverse * signal
    margin = jnp.sum(sign[...] * rewards, axis=1, keepdims=True)
    pairs = count // 2
    slope = -jax.nn.sigmoid(-margin) / pairs
    reward_slope = jnp.sum(sign[...] * slope, axis=0, keepdims=True)
    direct = reward_slope * inverse
    norm = direct * inverse * inverse * signal / D
    eye = lax.broadcasted_iota(jnp.int32, (HD, HD), 0) == lax.broadcasted_iota(
        jnp.int32, (HD, HD), 1
    )

    def upright(line):
        return jnp.concatenate(
            [
                jnp.sum(
                    jnp.where(eye, line[:, a * HD : (a + 1) * HD], 0.0), axis=1, keepdims=True
                )
                for a in range(lines)
            ],
            axis=0,
        )

    direct_rows = upright(direct)
    norm_rows = upright(norm)
    for c in range(chunks):
        here = pl.ds(c * mixed, mixed)
        part = (
            direct_rows[c * mixed : (c + 1) * mixed] * scaled_head
            - norm_rows[c * mixed : (c + 1) * mixed] * combined[here, :]
        ).astype(jnp.bfloat16)
        upstream[here, :] = part
        part = jnp.dot(turn[...], part, preferred_element_type=jnp.float32).astype(jnp.bfloat16)
        for k in range(groups):
            turned[k // chips, pl.ds(k % chips * held_count + c * block, block), :] = part[
                k * block : (k + 1) * block
            ]
    halves = near_send.shape[0]
    half = width // halves
    nears = []
    for k in range(halves):
        near_send[k] = lax.dot_general(
            turned[1 - core],
            w[k * half : (k + 1) * half, :],
            NT,
            preferred_element_type=jnp.float32,
        ).astype(jnp.bfloat16)
        copy = remote(near_send.at[k], near_land.at[k], near_sem, (k,), dp=sibling)
        copy.start()
        nears.append(copy)
    fars = []
    for k in range(halves):
        slopes = own.at[pl.ds(0, chips * held_count), pl.ds(0, half)]
        slopes[...] = lax.dot_general(
            turned[core],
            w[k * half : (k + 1) * half, :],
            NT,
            preferred_element_type=jnp.float32,
        )
        nears[k].wait_recv()
        for q in range(chips):
            goal = (chip + q) % chips
            there = at(goal * held_count, held_count)
            both = slopes[there, :] + near_land[k, there, :].astype(jnp.float32)
            if q == 0:
                reduced[:, k * half : (k + 1) * half] = both
            else:
                far_send[k, q - 1] = both.astype(jnp.bfloat16)
                copy = remote(
                    far_send.at[k, q - 1],
                    far_land.at[k, q - 1],
                    far_sem,
                    (k * (chips - 1) + q - 1,),
                    dp=goal * 2 + core,
                )
                copy.start()
                fars.append(copy)

    rewards_rows = upright(rewards)
    rewards_out[...] = jnp.sum(
        place[...].astype(jnp.float32) * rewards_rows, axis=0, keepdims=True
    )
    against = -margin
    soft = jnp.maximum(against, 0.0) + jnp.log1p(jnp.exp(-jnp.abs(against)))
    loss_out[...] = jnp.sum(soft, axis=0, keepdims=True) / pairs
    head_gradient[...] = jnp.sum(direct_rows * combined[...], axis=0, keepdims=True) * gain[...]

    for k in range(halves):
        extra = None
        for q in range(1, chips):
            fars[k * (chips - 1) + q - 1].wait_recv()
            piece = far_land[k, q - 1].astype(jnp.float32)
            extra = piece if extra is None else extra + piece
        reduced[:, k * half : (k + 1) * half] += extra

    for copy in backs:
        copy.wait_recv()
    for copy in locals_[chunks:]:
        copy.wait()
    sent = infos + backs + stats + nears + fars
    for group in moves + pools + passes:
        sent = sent + group
    for copy in sent + z_copies:
        copy.wait_send()

    @pl.when(depth > 0)
    def _():
        for copy in t_copies:
            copy.wait_send()


def gradient_kernel(per, chunk_slots, target, lengths, returned, reduced, pooled, upstream, rows_out, pooled_gradient, weight_gradient):
    groups = returned.shape[0] // per
    block = groups * chunk_slots

    @pl.when(pl.program_id(0) == 0)
    def _():
        token = lax.broadcasted_iota(jnp.int32, returned.shape[1:], 0)

        def body(r, carry):
            p = target[r]
            rows_out[r] = jnp.where(token < lengths[r], returned[p], jnp.zeros_like(returned[p]))
            owner = p // per
            j = p % per
            row = j // chunk_slots * block + owner * chunk_slots + j % chunk_slots
            pooled_gradient[pl.ds(r, 1), :] = reduced[pl.ds(row, 1), :]
            return carry

        lax.fori_loop(0, rows_out.shape[0], body, 0)

    weight_gradient[...] = lax.dot_general(
        pooled[...], upstream[...], TN, preferred_element_type=jnp.float32
    )


def fused_shards(
    response_query,
    response_keys,
    prompt_cache,
    lengths,
    owners,
    pairing,
    residual,
    output_weight,
    norm_gain,
    reward_head,
):
    groups = lax.axis_size("dp")
    planes = lax.axis_size("mp")
    held_count, slot_count, width = response_query.shape
    local_heads = width // HD
    group_size = Q_HEADS // KV_HEADS
    per = held_count // groups
    count = held_count * groups
    columns = output_weight.shape[1]
    prefix = prompt_cache.shape[2]
    window = kv_window(planes, local_heads)
    chunk_slots = slots_of_chunk(groups, per)
    chunks = per // chunk_slots
    block = groups * chunk_slots
    chips = groups // 2
    span = window * HD
    packed_width = width + 2 * span
    bf16, f32 = jnp.bfloat16, jnp.float32
    vmem = pl.BlockSpec(memory_space=pltpu.VMEM)
    smem = pl.BlockSpec(memory_space=pltpu.SMEM)
    hbm = pl.BlockSpec(memory_space=pltpu.HBM)
    packed, info, target = pl.pallas_call(
        functools.partial(plan_kernel, per, chunk_slots, window),
        out_shape=(
            jax.ShapeDtypeStruct((held_count, slot_count, packed_width), bf16),
            jax.ShapeDtypeStruct((groups, 16, HD), f32),
            jax.ShapeDtypeStruct((held_count,), jnp.int32),
        ),
        in_specs=[smem, smem, hbm, hbm],
        out_specs=(vmem, vmem, smem),
        scratch_shapes=[
            pltpu.SMEM((groups,), jnp.int32),
            pltpu.VMEM((held_count, slot_count, width), bf16),
            pltpu.VMEM((2, held_count, slot_count, span), bf16),
            pltpu.SemaphoreType.DMA((3,)),
        ],
        compiler_params=pltpu.CompilerParams(vmem_limit_bytes=16 << 20),
        name="plan",
    )(owners, lengths, response_query, response_keys)
    slots = held_count * slot_count
    sub = SUB
    steps = count // sub
    halves = 2
    half = width // halves
    dma = lambda *shape: pltpu.SemaphoreType.DMA(shape)
    returned, pooled, upstream, reduced, head_gradient, rewards, loss = pl.pallas_call(
        functools.partial(
            layer_kernel, (groups, planes, per, chunk_slots, window, sub)
        ),
        out_shape=(
            jax.ShapeDtypeStruct((slots, width), bf16),
            jax.ShapeDtypeStruct((count, width), bf16),
            jax.ShapeDtypeStruct((count, columns), bf16),
            jax.ShapeDtypeStruct((held_count, width), f32),
            jax.ShapeDtypeStruct((1, columns), f32),
            jax.ShapeDtypeStruct((1, count), f32),
            jax.ShapeDtypeStruct((1, 1), f32),
        ),
        in_specs=[vmem, vmem, hbm, hbm, hbm, vmem, vmem, vmem],
        out_specs=(vmem,) * 7,
        scratch_shapes=[
            pltpu.VMEM((slots, packed_width), bf16),
            pltpu.VMEM((groups, 16, HD), f32),
            pltpu.VMEM((2, prefix, span), bf16),
            pltpu.VMEM((width, columns), bf16),
            pltpu.VMEM((count, columns), bf16),
            pltpu.VMEM((count, count), bf16),
            pltpu.VMEM((count // 2, count), f32),
            pltpu.VMEM((groups * block, groups * block), bf16),
            pltpu.VMEM((count, columns), f32),
            pltpu.VMEM((slots, width), bf16),
            pltpu.VMEM((count, columns), f32),
            pltpu.VMEM((count, columns), bf16),
            pltpu.VMEM((2, count, columns), bf16),
            pltpu.VMEM((count, columns), bf16),
            pltpu.VMEM((count, columns), f32),
            pltpu.VMEM((8, HD), f32),
            pltpu.VMEM((groups, 8, HD), f32),
            pltpu.VMEM((2, chips * held_count, columns), bf16),
            pltpu.VMEM((halves, chips * held_count, half), bf16),
            pltpu.VMEM((halves, chips * held_count, half), bf16),
            pltpu.VMEM((halves, chips - 1, held_count, half), bf16),
            pltpu.VMEM((halves, chips - 1, held_count, half), bf16),
            dma(4),
            dma(2, groups - 1),
            dma(2, chunks * (groups - 1)),
            dma(2 * chunks),
            dma(2, chunks * chips),
            dma(2, chunks * (chips - 1)),
            dma(2, chunks * (groups - 1)),
            dma(2, 2, steps),
            dma(2, steps),
            dma(2, groups - 1),
            dma(2, halves),
            dma(2, halves * (chips - 1)),
        ],
        compiler_params=pltpu.CompilerParams(
            collective_id=0, has_side_effects=True, vmem_limit_bytes=44 << 20
        ),
        name="layer",
    )(
        packed.reshape(slots, packed_width),
        info,
        prompt_cache,
        output_weight,
        residual,
        norm_gain[None],
        reward_head[None],
        pairing[None],
    )
    tile = 256
    attention_rows, pooled_gradient, weight_gradient = pl.pallas_call(
        functools.partial(gradient_kernel, per, chunk_slots),
        out_shape=(
            jax.ShapeDtypeStruct(response_query.shape, bf16),
            jax.ShapeDtypeStruct((held_count, width), f32),
            jax.ShapeDtypeStruct((width, columns), f32),
        ),
        grid=(width // tile,),
        in_specs=[
            smem,
            smem,
            pl.BlockSpec((held_count, slot_count, width), lambda i: (0, 0, 0)),
            pl.BlockSpec((held_count, width), lambda i: (0, 0)),
            pl.BlockSpec((count, tile), lambda i: (0, i)),
            pl.BlockSpec((count, columns), lambda i: (0, 0)),
        ],
        out_specs=(
            pl.BlockSpec((held_count, slot_count, width), lambda i: (0, 0, 0)),
            pl.BlockSpec((held_count, width), lambda i: (0, 0)),
            pl.BlockSpec((tile, columns), lambda i: (i, 0)),
        ),
        compiler_params=pltpu.CompilerParams(vmem_limit_bytes=32 << 20),
        name="gradient",
    )(
        target,
        lengths,
        returned.reshape(held_count, slot_count, width),
        reduced,
        pooled,
        upstream,
    )
    return (
        attention_rows,
        rewards[0],
        loss[0, 0],
        weight_gradient,
        head_gradient[0],
        pooled_gradient,
    )


SUB = 32


def kv_window(planes, local_heads):
    group_size = Q_HEADS // KV_HEADS
    return max(
        (m * local_heads + local_heads - 1) // group_size - m * local_heads // group_size + 1
        for m in range(planes)
    )


def slots_of_chunk(groups, per):
    for slots in range(1, per + 1):
        if per % slots == 0 and slots * groups % 16 == 0:
            return slots
    return 0


def fits(shape, responses):
    groups, planes = shape["dp"], shape["mp"]
    held = responses // groups
    if held % groups or groups % 2 or planes % 2:
        return False
    slots = slots_of_chunk(groups, held // groups)
    return bool(slots) and slots * groups * 8 == HD and responses % HD == 0 and responses <= 3 * HD


def shards(*args):
    held = args[0].shape[0]
    groups = lax.axis_size("dp")
    sizes = {"dp": groups, "mp": lax.axis_size("mp")}
    if fits(sizes, held * groups):
        return fused_shards(*args)
    return stepwise_shards(*args)


def solution(mesh):
    placed = (
        P("dp", None, "mp"),
        P(None, "dp", None, None),
        P(None, "dp", None, None),
        P("dp"),
        P("dp"),
        P(),
        P(None, "dp"),
        P("mp", "dp"),
        P("dp"),
        P("dp"),
    )
    return jax.shard_map(
        shards,
        mesh=mesh,
        in_specs=placed,
        out_specs=(P("dp", None, "mp"), P(), P(), P("mp", "dp"), P("dp"), P("dp", "mp")),
        check_vma=False,
    )
```

```python
import functools
import math

import jax
import jax.numpy as jnp
from jax import lax
from jax.experimental import pallas as pl
from jax.experimental.pallas import tpu as pltpu
from jax.sharding import PartitionSpec as P

D = 8192
HD = 128
Q_HEADS = 48
KV_HEADS = 6


EPSILON = 1e-05


def bradley_terry(rewards, pairing):
    count = rewards.shape[0]
    chosen = pairing[0::2, None] == jnp.arange(count)[None, :]
    rejected = pairing[1::2, None] == jnp.arange(count)[None, :]
    sign = chosen.astype(jnp.float32) - rejected.astype(jnp.float32)
    margin = jnp.sum(sign * rewards[None, :], axis=1)
    loss_value = jnp.mean(jax.nn.softplus(-margin))
    slope = -jax.nn.sigmoid(-margin) / margin.shape[0]
    reward_slope = jnp.sum(sign * slope[:, None], axis=0)
    return (loss_value, reward_slope)


def pack_kernel(window, meta, query, keys, out, late):
    slots = out.shape[0]
    rest = late.shape[2]
    width = query.shape[2] - rest
    span = window * HD
    first = pl.multiple_of(meta[2 * slots] * HD, HD)

    def body(p, carry):
        r = meta[p]
        out[p, :, pl.ds(0, width)] = query[r, :, pl.ds(0, width)]
        late[p] = query[r, :, pl.ds(width, rest)]
        out[p, :, pl.ds(width, span)] = keys[0, r, :, pl.ds(first, span)]
        out[p, :, pl.ds(width + span, span)] = keys[1, r, :, pl.ds(first, span)]
        length = meta[slots + p].astype(jnp.float32)
        place = r.astype(jnp.float32)
        lane = lax.broadcasted_iota(jnp.int32, (out.shape[1], HD), 1)
        out[p, :, pl.ds(width + 2 * span, HD)] = jnp.where(lane < HD // 2, length, place).astype(
            jnp.bfloat16
        )
        return carry

    lax.fori_loop(0, slots, body, 0)


def attention_kernel(slot_count, placed, meta, query, own_k, own_v, lens, cache, out, pooled):
    rows = query.shape[0]
    head = pl.program_id(0)
    chunk = 128
    blocks = chunk // slot_count
    scale = math.log2(math.e) / math.sqrt(HD)
    contract = (((1,), (1,)), ((), ()))
    row = lax.broadcasted_iota(jnp.int32, (chunk, chunk), 0)
    col = lax.broadcasted_iota(jnp.int32, (chunk, chunk), 1)
    t = row % slot_count
    s = col % slot_count
    causal = (row // slot_count == col // slot_count) & (s <= t)
    s_float = s.astype(jnp.float32)
    t_float = t.astype(jnp.float32)
    gather = lax.broadcasted_iota(jnp.int32, (blocks, chunk), 0)
    member = lax.broadcasted_iota(jnp.int32, (blocks, chunk), 1)
    gather = jnp.where(gather == member // slot_count, 1.0, 0.0).astype(jnp.bfloat16)
    for start in range(0, rows, chunk):
        here = pl.ds(start, chunk)
        q = query[here, :]
        length = jnp.broadcast_to(lens[here, :].astype(jnp.float32)[:, 0:1], (chunk, chunk))
        far = lax.dot_general(q, cache[0, 0], contract, preferred_element_type=jnp.float32)
        near = lax.dot_general(q, own_k[here, :], contract, preferred_element_type=jnp.float32)
        near = jnp.where(causal & (s_float < length), near, -jnp.inf)
        top = jnp.maximum(
            jnp.max(far, axis=1, keepdims=True), jnp.max(near, axis=1, keepdims=True)
        )
        far = jnp.exp2((far - top) * scale)
        near = jnp.exp2((near - top) * scale)
        total = jnp.sum(far, axis=1, keepdims=True) + jnp.sum(near, axis=1, keepdims=True)
        value = jnp.dot(far.astype(jnp.bfloat16), cache[1, 0], preferred_element_type=jnp.float32)
        value += jnp.dot(
            near.astype(jnp.bfloat16), own_v[here, :], preferred_element_type=jnp.float32
        )
        value = jnp.where(t_float < length, value / total, 0.0)
        out[here, :] = value.astype(jnp.bfloat16)
        last = jnp.where(t_float == length - 1.0, value, 0.0)
        last = jnp.dot(gather, last.astype(jnp.bfloat16), preferred_element_type=jnp.float32)
        there = pl.ds(start // slot_count, blocks)
        pooled[there, pl.ds(pl.multiple_of(head * HD, HD), HD)] = last.astype(jnp.bfloat16)

        if placed:

            @pl.when(head == 0)
            def _():
                place = lens[here, :].astype(jnp.float32).reshape(blocks, slot_count, HD)
                pooled[there, pl.ds(pooled.shape[1] - HD, HD)] = jnp.max(place, axis=1).astype(
                    jnp.bfloat16
                )


def unpack_kernel(meta, returned, out):
    def body(r, carry):
        out[r] = returned[meta[r]]
        return carry

    lax.fori_loop(0, out.shape[0], body, 0)


def stepwise_shards(
    response_query,
    response_keys,
    prompt_cache,
    lengths,
    owners,
    pairing,
    residual,
    output_weight,
    norm_gain,
    reward_head,
):
    groups = lax.axis_size("dp")
    planes = lax.axis_size("mp")
    model_rank = lax.axis_index("mp")
    held_count, slot_count, head_width = response_query.shape
    local_heads = head_width // HD
    group_size = Q_HEADS // KV_HEADS
    per_owner = (held_count + groups - 1) // groups
    capacity = groups * per_owner
    window = max(
        (m * local_heads + local_heads - 1) // group_size - m * local_heads // group_size + 1
        for m in range(planes)
    )
    first_head = jnp.minimum(model_rank * local_heads // group_size, KV_HEADS - window)
    head_kv = (model_rank * local_heads + jnp.arange(local_heads)) // group_size
    positions = jnp.arange(held_count)
    earlier = (owners[None, :] == owners[:, None]) & (positions[None, :] < positions[:, None])
    target = (owners * per_owner + jnp.sum(earlier, axis=1)).astype(jnp.int32)
    sent_from = (target[None, :] == jnp.arange(capacity)[:, None]).astype(jnp.int32)
    source = jnp.sum(sent_from * positions[None, :], axis=1)
    slot_length = jnp.sum(sent_from * lengths[None, :], axis=1)
    params = pltpu.CompilerParams(vmem_limit_bytes=40 * 1024 * 1024)
    vmem = pl.BlockSpec(memory_space=pltpu.VMEM)
    smem = pl.BlockSpec(memory_space=pltpu.SMEM)
    early = local_heads - local_heads // 2
    late_width = local_heads // 2 * HD
    packed_width = early * HD + (2 * window + 1) * HD
    packed, late = pl.pallas_call(
        functools.partial(pack_kernel, window),
        out_shape=(
            jax.ShapeDtypeStruct((capacity, slot_count, packed_width), jnp.bfloat16),
            jax.ShapeDtypeStruct((capacity, slot_count, late_width), jnp.bfloat16),
        ),
        in_specs=[smem, vmem, vmem],
        out_specs=(vmem, vmem),
        compiler_params=params,
        name="pack",
    )(
        jnp.concatenate([source, slot_length, first_head[None]]).astype(jnp.int32),
        response_query,
        response_keys,
    )
    packed = packed.reshape(groups, per_owner, slot_count, packed_width)
    arrived = lax.all_to_all(packed, "dp", split_axis=0, concat_axis=0, tiled=True)
    late = late.reshape(groups, per_owner, slot_count, late_width)
    late = lax.all_to_all(late, "dp", split_axis=0, concat_axis=0, tiled=True)
    rows = capacity * slot_count
    late = late.reshape(rows, late_width)
    arrived = arrived.reshape(rows, packed_width)
    block = (rows, HD)

    def attend(query, head_base, heads, placed):
        pooled_width = (heads + placed) * HD
        at = lambda meta, h: meta[local_heads + head_base + h]
        return pl.pallas_call(
            functools.partial(attention_kernel, slot_count, placed),
            out_shape=(
                jax.ShapeDtypeStruct((rows, heads * HD), jnp.bfloat16),
                jax.ShapeDtypeStruct((capacity, pooled_width), jnp.bfloat16),
            ),
            grid_spec=pltpu.PrefetchScalarGridSpec(
                num_scalar_prefetch=1,
                grid=(heads,),
                in_specs=[
                    pl.BlockSpec(block, lambda h, meta: (0, h)),
                    pl.BlockSpec(block, lambda h, meta: (0, early + at(meta, h))),
                    pl.BlockSpec(block, lambda h, meta: (0, early + window + at(meta, h))),
                    pl.BlockSpec(block, lambda h, meta: (0, early + 2 * window)),
                    pl.BlockSpec(
                        (2, 1, prompt_cache.shape[2], HD),
                        lambda h, meta: (0, 0, 0, meta[head_base + h]),
                    ),
                ],
                out_specs=(
                    pl.BlockSpec(block, lambda h, meta: (0, h)),
                    pl.BlockSpec((capacity, pooled_width), lambda h, meta: (0, 0)),
                ),
            ),
            compiler_params=params,
            cost_estimate=pl.CostEstimate(
                flops=4 * rows * heads * HD * prompt_cache.shape[2],
                bytes_accessed=8 * rows * heads * HD,
                transcendentals=rows * heads * prompt_cache.shape[2],
            ),
            name="attention_early" if placed else "attention_late",
        )(
            jnp.concatenate([head_kv, head_kv - first_head]).astype(jnp.int32),
            query,
            arrived,
            arrived,
            arrived,
            prompt_cache,
        )

    def share_rows(own):
        copies = jnp.broadcast_to(own[None], (groups,) + own.shape)
        copies = lax.all_to_all(copies, "dp", split_axis=0, concat_axis=0, tiled=True)
        return copies.reshape(groups * own.shape[0], own.shape[1])

    attended_early, pooled_early = attend(arrived, 0, early, True)
    pooled_slots = share_rows(pooled_early)
    attended_late, pooled_late = attend(late, early, local_heads - early, False)
    pooled_late = share_rows(pooled_late)
    attended = jnp.concatenate([attended_early, attended_late], axis=1)
    result = attended.reshape(groups, per_owner, slot_count, head_width)
    returned = lax.all_to_all(result, "dp", split_axis=0, concat_axis=0, tiled=True)
    attention_rows = pl.pallas_call(
        unpack_kernel,
        out_shape=jax.ShapeDtypeStruct(response_query.shape, jnp.bfloat16),
        in_specs=[smem, vmem],
        out_specs=vmem,
        compiler_params=params,
        name="unpack",
    )(target, returned.reshape(capacity, slot_count, head_width))
    count = held_count * groups
    sender = jnp.arange(capacity * groups) % capacity // per_owner
    place = pooled_slots[:, early * HD + HD - 1].astype(jnp.int32)
    live = pooled_slots[:, early * HD] > 0
    response = jnp.where(live, sender * held_count + place, count)
    order = (jnp.arange(count)[:, None] == response[None, :]).astype(jnp.bfloat16)
    pooled_all = jnp.concatenate(
        [
            jnp.dot(order, slots, preferred_element_type=jnp.float32).astype(jnp.bfloat16)
            for slots in (pooled_slots[:, : early * HD], pooled_late)
        ],
        axis=1,
    )
    share = count // planes
    partial_mix = jnp.dot(pooled_all, output_weight, preferred_element_type=jnp.float32)
    columns = output_weight.shape[1]
    scaled_head = norm_gain * reward_head
    shares = lax.all_to_all(
        partial_mix.astype(jnp.bfloat16).reshape(planes, share, columns),
        "mp",
        split_axis=0,
        concat_axis=0,
        tiled=True,
    )
    part = jnp.sum(shares.astype(jnp.float32), axis=0) + lax.dynamic_slice_in_dim(
        residual, model_rank * share, share, 0
    ).astype(jnp.float32)
    combined = lax.all_gather(part.astype(jnp.bfloat16), "mp", axis=0, tiled=True).astype(
        jnp.float32
    )
    square_sum = jnp.sum(combined * combined, axis=1)
    signal = jnp.sum(combined * scaled_head[None, :], axis=1)
    square_sum, signal = lax.psum((square_sum, signal), "dp")
    inverse = lax.rsqrt(square_sum / D + EPSILON)
    rewards = inverse * signal
    pair_loss, reward_slope = bradley_terry(rewards, pairing)
    direct_term = reward_slope * inverse
    norm_term = reward_slope * inverse * inverse * inverse * signal / D
    upstream = direct_term[:, None] * scaled_head[None, :] - norm_term[:, None] * combined
    head_gradient = jnp.sum(direct_term[:, None] * combined * norm_gain[None, :], axis=0)
    upstream_half = upstream.astype(jnp.bfloat16)
    slope_part = lax.dot_general(
        upstream_half,
        output_weight,
        (((1,), (1,)), ((), ())),
        preferred_element_type=jnp.float32,
    ).astype(jnp.bfloat16)
    slope_parts = lax.all_to_all(
        slope_part.reshape(groups, held_count, head_width),
        "dp",
        split_axis=0,
        concat_axis=0,
        tiled=True,
    )
    weight_gradient = lax.dot_general(
        pooled_all, upstream_half, (((0,), (0,)), ((), ())), preferred_element_type=jnp.float32
    )
    pooled_gradient = jnp.sum(slope_parts.astype(jnp.float32), axis=0)
    return (attention_rows, rewards, pair_loss, weight_gradient, head_gradient, pooled_gradient)


MESH = pl.DeviceIdType.MESH
NT = (((1,), (1,)), ((), ()))
TN = (((0,), (0,)), ((), ()))


def plan_kernel(per, chunk_slots, window, owners, lengths, query, keys, packed, info, target, count, got, held, sems):
    me = lax.axis_index("dp")
    groups = count.shape[0]
    held_count = query.shape[0]
    width = query.shape[2]
    span = window * HD
    first = jnp.minimum(
        lax.axis_index("mp") * (width // HD) // (Q_HEADS // KV_HEADS), KV_HEADS - window
    )
    columns = pl.ds(pl.multiple_of(first * HD, HD), span)
    loads = [
        pltpu.make_async_copy(query, got, sems.at[0]),
        pltpu.make_async_copy(keys.at[0, :, :, columns], held.at[0], sems.at[1]),
        pltpu.make_async_copy(keys.at[1, :, :, columns], held.at[1], sems.at[2]),
    ]
    for load in loads:
        load.start()
    for owner in range(groups):
        count[owner] = 0
    spot = lax.broadcasted_iota(jnp.int32, (8, HD), 0) * HD + lax.broadcasted_iota(
        jnp.int32, (8, HD), 1
    )
    block = groups * chunk_slots

    def place(r, rows):
        owner = owners[r]
        j = count[owner]
        count[owner] = j + 1
        target[r] = owner * per + j
        info[owner, pl.ds(j, 1), :] = jnp.full((1, HD), lengths[r], jnp.int32).astype(jnp.float32)
        row = (
            j // chunk_slots * (groups * block) + owner * block + j % chunk_slots * groups + me
        )
        return jnp.where(spot == me * held_count + r, row, rows)

    rows = lax.fori_loop(0, held_count, place, jnp.zeros((8, HD), jnp.int32))
    for owner in range(groups):
        info[owner, pl.ds(8, 8), :] = rows.astype(jnp.float32)
    for load in loads:
        load.wait()

    def move(r, carry):
        p = target[r]
        packed[p, :, pl.ds(0, width)] = got[r]
        packed[p, :, pl.ds(width, span)] = held[0, r]
        packed[p, :, pl.ds(width + span, span)] = held[1, r]
        return carry

    lax.fori_loop(0, held_count, move, 0)


def layer_kernel(
    sizes,
    packed,
    info,
    cache,
    weight,
    residual,
    gain,
    head,
    pairing,
    returned,
    pooled,
    upstream,
    reduced,
    head_gradient,
    rewards_out,
    loss_out,
    land,
    info_land,
    kv,
    w,
    res,
    place,
    sign,
    turn,
    shifted,
    attended,
    own,
    z_send,
    z_land,
    z_total,
    combined,
    stat,
    stat_land,
    turned,
    near_send,
    near_land,
    far_send,
    far_land,
    load_sem,
    info_sem,
    move_sem,
    local_sem,
    pool_sem,
    pass_sem,
    back_sem,
    z_sem,
    t_sem,
    stat_sem,
    near_sem,
    far_sem,
):
    groups, planes, per, chunk_slots, window, sub = sizes
    held_count = reduced.shape[0]
    me = lax.axis_index("dp")
    rank = lax.axis_index("mp")
    chips = groups // 2
    chip = me // 2
    core = me % 2
    sibling = chip * 2 + 1 - core
    chunks = per // chunk_slots
    block = groups * chunk_slots
    unit = chunk_slots * 8
    rows = block * 8
    mixed = groups * block
    width = attended.shape[1]
    local_heads = width // HD
    group_size = Q_HEADS // KV_HEADS
    stack = math.gcd(local_heads, group_size)
    span = window * HD
    count = pooled.shape[0]
    first = jnp.minimum(rank * local_heads // group_size, KV_HEADS - window)
    columns = pl.ds(pl.multiple_of(first * HD, HD), span)

    def remote(src, dst, sem, index, **where):
        return pltpu.make_async_remote_copy(
            src_ref=src,
            dst_ref=dst,
            send_sem=sem.at[(0,) + index],
            recv_sem=sem.at[(1,) + index],
            device_id=where,
            device_id_type=MESH,
        )

    def at(start, size):
        return pl.ds(pl.multiple_of(start, size), size)

    loads = [
        pltpu.make_async_copy(cache.at[0, 0, :, columns], kv.at[0], load_sem.at[0]),
        pltpu.make_async_copy(cache.at[1, 0, :, columns], kv.at[1], load_sem.at[1]),
        pltpu.make_async_copy(residual, res, load_sem.at[2]),
        pltpu.make_async_copy(weight, w, load_sem.at[3]),
    ]
    for load in loads:
        load.start()

    barrier = pltpu.get_barrier_semaphore()
    for d in range(1, groups):
        pl.semaphore_signal(
            barrier, inc=1, device_id={"dp": (me + d) % groups}, device_id_type=MESH
        )
    for d in range(1, planes):
        pl.semaphore_signal(
            barrier, inc=1, device_id={"mp": (rank + d) % planes}, device_id_type=MESH
        )
    pl.semaphore_wait(barrier, groups + planes - 2)

    infos = []
    for d in range(1, groups):
        peer = (me + d) % groups
        copy = remote(info.at[peer], info_land.at[me], info_sem, (d - 1,), dp=peer)
        copy.start()
        infos.append(copy)
    moves = []
    locals_ = []

    def dispatch(c):
        moves.append([])
        for d in range(1, groups):
            peer = (me + d) % groups
            copy = remote(
                packed.at[at((peer * chunks + c) * unit, unit), :],
                land.at[at((c * groups + me) * unit, unit), :],
                move_sem,
                (c * (groups - 1) + d - 1,),
                dp=peer,
            )
            copy.start()
            moves[c].append(copy)
        copy = pltpu.make_async_copy(
            packed.at[at((me * chunks + c) * unit, unit), :],
            land.at[at((c * groups + me) * unit, unit), :],
            local_sem.at[c],
        )
        copy.start()
        locals_.append(copy)

    dispatch(0)

    info_land[me] = info[me]
    for copy in infos:
        copy.wait_recv()
    row_of = info_land[0, pl.ds(8, 8), :]
    for g in range(1, groups):
        row_of = row_of + info_land[g, pl.ds(8, 8), :]
    row_of = row_of.astype(jnp.int32)
    row_at = lax.broadcasted_iota(jnp.int32, (count, HD), 0)
    for a in range(count // HD):
        place[:, a * HD : (a + 1) * HD] = jnp.where(
            row_at == row_of[a : a + 1, :], 1.0, 0.0
        ).astype(jnp.bfloat16)
    asked = jnp.where(
        lax.broadcasted_iota(jnp.int32, (count, count), 0) == pairing[...], 1.0, 0.0
    ).astype(jnp.bfloat16)
    pair = lax.broadcasted_iota(jnp.int32, (count // 2, count), 0) * 2
    entry = lax.broadcasted_iota(jnp.int32, (count // 2, count), 1)
    side = jnp.where(entry == pair, 1.0, jnp.where(entry == pair + 1, -1.0, 0.0))
    chosen = lax.dot_general(
        side.astype(jnp.bfloat16), asked, NT, preferred_element_type=jnp.float32
    )
    sign[...] = lax.dot_general(
        chosen.astype(jnp.bfloat16), place[...], NT, preferred_element_type=jnp.float32
    )
    loads[2].wait()
    shifted[...] = jnp.dot(place[...], res[...], preferred_element_type=jnp.float32)

    new = lax.broadcasted_iota(jnp.int32, (mixed, mixed), 0)
    old = lax.broadcasted_iota(jnp.int32, (mixed, mixed), 1)
    old_at = new % block * groups + new // block % chips * 2 + new // (block * chips)
    turn[...] = jnp.where(old == old_at, 1.0, 0.0).astype(jnp.bfloat16)

    scale = math.log2(math.e) / math.sqrt(HD)
    tall = stack * rows

    def attend(c):
        here = pl.ds(c * rows, rows)
        row = lax.broadcasted_iota(jnp.int32, (tall, rows), 0) % rows
        col = lax.broadcasted_iota(jnp.int32, (tall, rows), 1)
        causal = (row // 8 == col // 8) & (col <= row)
        for s in range(local_heads // stack):
            part = (rank * local_heads + stack * s) // group_size - first
            query = jnp.concatenate(
                [
                    land[here, h * HD : (h + 1) * HD]
                    for h in range(s * stack, (s + 1) * stack)
                ],
                axis=0,
            )
            own_k = land[here, pl.ds(pl.multiple_of(width + part * HD, HD), HD)]
            own_v = land[here, pl.ds(pl.multiple_of(width + span + part * HD, HD), HD)]
            key = kv[0, :, pl.ds(pl.multiple_of(part * HD, HD), HD)]
            value = kv[1, :, pl.ds(pl.multiple_of(part * HD, HD), HD)]
            far = lax.dot_general(query, key, NT, preferred_element_type=jnp.float32)
            near = lax.dot_general(query, own_k, NT, preferred_element_type=jnp.float32)
            near = jnp.where(causal, near, -1e30)
            top = jnp.maximum(
                jnp.max(far, axis=1, keepdims=True), jnp.max(near, axis=1, keepdims=True)
            )
            far = jnp.exp2((far - top) * scale).astype(jnp.bfloat16)
            near = jnp.exp2((near - top) * scale).astype(jnp.bfloat16)
            ones = lambda v: jnp.concatenate([v, jnp.ones_like(v)], axis=1)
            both = jnp.dot(far, ones(value), preferred_element_type=jnp.float32)
            both += jnp.dot(near, ones(own_v), preferred_element_type=jnp.float32)
            out = (both[:, :HD] / both[:, HD:]).astype(jnp.bfloat16)
            for h in range(stack):
                attended[here, (s * stack + h) * HD : (s * stack + h + 1) * HD] = out[
                    h * rows : (h + 1) * rows
                ]

    pools = []
    passes = []

    def share(c):
        slots = [
            jnp.concatenate(
                [info_land[g, pl.ds(c * chunk_slots + k, 1), :] for g in range(groups)], axis=0
            )
            for k in range(chunk_slots)
        ]
        length = jnp.concatenate(slots, axis=0).astype(jnp.int32)
        i = lax.broadcasted_iota(jnp.int32, (block, HD), 0)
        col = lax.broadcasted_iota(jnp.int32, (block, HD), 1)
        start = (i % groups * chunk_slots + i // groups) * 8 - 1
        pick = jnp.where(col == start + length, 1.0, 0.0).astype(jnp.bfloat16)
        last = jnp.dot(
            pick, attended[pl.ds(c * rows, rows), :], preferred_element_type=jnp.float32
        )
        mine = at(c * mixed + me * block, block)
        pooled[mine, :] = last.astype(jnp.bfloat16)
        sent = []
        for q in range(1, chips):
            sent.append(
                remote(
                    pooled.at[mine, :],
                    pooled.at[mine, :],
                    pool_sem,
                    (c * chips + q,),
                    dp=(chip + q) % chips * 2 + core,
                )
            )
        sent.append(
            remote(
                pooled.at[mine, :], pooled.at[mine, :], pool_sem, (c * chips,), dp=sibling
            )
        )
        for copy in sent:
            copy.start()
        pools.append(sent)

    def pass_on(c):
        sent = []
        for q in range(1, chips):
            pools[c][q - 1].wait_recv()
            source = (chip + chips - q) % chips * 2 + core
            there = at(c * mixed + source * block, block)
            copy = remote(
                pooled.at[there, :],
                pooled.at[there, :],
                pass_sem,
                (c * (chips - 1) + q - 1,),
                dp=sibling,
            )
            copy.start()
            sent.append(copy)
        passes.append(sent)

    depth = jnp.minimum(rank, planes - 1 - rank)
    centre = planes // 2 - 1
    is_centre = depth == centre
    low = rank < planes // 2
    inward = jnp.where(low, rank + 1, rank - 1)
    outward = jnp.where(low, rank - 1, rank + 1)
    outward = jnp.where(depth == 0, inward, outward)
    slot = jnp.where(is_centre, 1, 0)
    steps = mixed // sub
    z_copies = [
        remote(
            z_send.at[pl.ds(n * sub, sub), :],
            z_land.at[slot, pl.ds(n * sub, sub), :],
            z_sem,
            (slot, n),
            mp=inward,
        )
        for n in range(chunks * steps)
    ]
    z_waits = [
        [
            remote(
                z_send.at[pl.ds(n * sub, sub), :],
                z_land.at[k, pl.ds(n * sub, sub), :],
                z_sem,
                (k, n),
                mp=inward,
            )
            for n in range(chunks * steps)
        ]
        for k in range(2)
    ]
    t_copies = [
        remote(
            z_total.at[pl.ds(n * sub, sub), :],
            z_total.at[pl.ds(n * sub, sub), :],
            t_sem,
            (n,),
            mp=outward,
        )
        for n in range(chunks * steps)
    ]

    def mix(c):
        for copy in passes[c]:
            copy.wait_recv()
        pools[c][-1].wait_recv()
        if c == 0:
            loads[3].wait()
        here = pl.ds(c * mixed, mixed)
        product = jnp.dot(pooled[here, :], w[...], preferred_element_type=jnp.float32)
        own[here, :] = product
        z_send[here, :] = product.astype(jnp.bfloat16)

        @pl.when(depth == 0)
        def _():
            for n in range(c * steps, (c + 1) * steps):
                z_copies[n].start()

    def inner(n):
        here = pl.ds(n * sub, sub)

        @pl.when(depth > 0)
        def _():
            z_waits[0][n].wait_recv()
            z_send[here, :] = (own[here, :] + z_land[0, here, :].astype(jnp.float32)).astype(
                jnp.bfloat16
            )
            z_copies[n].start()

    scaled_head = gain[...] * head[...]

    def finish(n):
        here = pl.ds(n * sub, sub)

        @pl.when(is_centre)
        def _():
            z_waits[1][n].wait_recv()
            z_total[here, :] = (
                z_send[here, :].astype(jnp.float32) + z_land[1, here, :].astype(jnp.float32)
            ).astype(jnp.bfloat16)

        @pl.when(depth < centre)
        def _():
            t_copies[n].wait_recv()

        @pl.when(depth > 0)
        def _():
            t_copies[n].start()

        whole = z_total[here, :].astype(jnp.float32) + shifted[here, :]
        combined[here, :] = whole
        square = jnp.sum(whole * whole, axis=1, keepdims=True)
        signal = jnp.sum(whole * scaled_head, axis=1, keepdims=True)
        lane = lax.broadcasted_iota(jnp.int32, (sub, HD), 1)
        this = lax.broadcasted_iota(jnp.int32, (sub, HD), 0) + n * sub % HD
        line = n * sub // HD
        for k, column in enumerate((square, signal)):
            spread = jnp.sum(jnp.where(lane == this, column, 0.0), axis=0, keepdims=True)
            there = pl.ds(k * (count // HD) + line, 1)
            if n * sub % HD == 0:
                stat[there, :] = spread
            else:
                stat[there, :] += spread

    backs = []

    def give_back(c):
        for d in range(1, groups):
            peer = (me + d) % groups
            copy = remote(
                attended.at[at((c * groups + peer) * unit, unit), :],
                returned.at[at((me * chunks + c) * unit, unit), :],
                back_sem,
                (c * (groups - 1) + d - 1,),
                dp=peer,
            )
            copy.start()
            backs.append(copy)
        copy = pltpu.make_async_copy(
            attended.at[at((c * groups + me) * unit, unit), :],
            returned.at[at((me * chunks + c) * unit, unit), :],
            local_sem.at[chunks + c],
        )
        copy.start()
        locals_.append(copy)

    for c in range(chunks):
        for copy in moves[c]:
            copy.wait_recv()
        locals_[c].wait()
        if c + 1 < chunks:
            dispatch(c + 1)
        if c == 0:
            loads[0].wait()
            loads[1].wait()
        attend(c)
        share(c)
        if c == chunks - 1:
            for n in range((chunks - 2) * steps):
                inner(n)
        if c > 0:
            pass_on(c - 1)
            mix(c - 1)
    taken = (chunks - 2) * steps
    pass_on(chunks - 1)
    for c in range(chunks):
        give_back(c)
    mix(chunks - 1)
    total = chunks * steps
    done = 0
    for n in range(taken, total):
        inner(n)
        while done < n - 1 + (n == total - 1):
            finish(done)
            done += 1
    while done < total:
        finish(done)
        done += 1

    lines = count // HD
    stat[pl.ds(2 * lines, 8 - 2 * lines), :] = jnp.zeros((8 - 2 * lines, HD), jnp.float32)
    stats = []
    for d in range(1, groups):
        copy = remote(stat, stat_land.at[me], stat_sem, (d - 1,), dp=(me + d) % groups)
        copy.start()
        stats.append(copy)
    stat_land[me] = stat[...]
    for copy in stats:
        copy.wait_recv()
    sums = stat_land[0]
    for g in range(1, groups):
        sums = sums + stat_land[g]
    square_sum = jnp.concatenate([sums[a : a + 1] for a in range(lines)], axis=1)
    signal = jnp.concatenate([sums[lines + a : lines + a + 1] for a in range(lines)], axis=1)
    inverse = lax.rsqrt(square_sum / D + EPSILON)
    rewards = inverse * signal
    margin = jnp.sum(sign[...] * rewards, axis=1, keepdims=True)
    pairs = count // 2
    slope = -jax.nn.sigmoid(-margin) / pairs
    reward_slope = jnp.sum(sign[...] * slope, axis=0, keepdims=True)
    direct = reward_slope * inverse
    norm = direct * inverse * inverse * signal / D
    eye = lax.broadcasted_iota(jnp.int32, (HD, HD), 0) == lax.broadcasted_iota(
        jnp.int32, (HD, HD), 1
    )

    def upright(line):
        return jnp.concatenate(
            [
                jnp.sum(
                    jnp.where(eye, line[:, a * HD : (a + 1) * HD], 0.0), axis=1, keepdims=True
                )
                for a in range(lines)
            ],
            axis=0,
        )

    direct_rows = upright(direct)
    norm_rows = upright(norm)
    for c in range(chunks):
        here = pl.ds(c * mixed, mixed)
        part = (
            direct_rows[c * mixed : (c + 1) * mixed] * scaled_head
            - norm_rows[c * mixed : (c + 1) * mixed] * combined[here, :]
        ).astype(jnp.bfloat16)
        upstream[here, :] = part
        part = jnp.dot(turn[...], part, preferred_element_type=jnp.float32).astype(jnp.bfloat16)
        for k in range(groups):
            turned[k // chips, pl.ds(k % chips * held_count + c * block, block), :] = part[
                k * block : (k + 1) * block
            ]
    halves = near_send.shape[0]
    half = width // halves
    nears = []
    for k in range(halves):
        near_send[k] = lax.dot_general(
            turned[1 - core],
            w[k * half : (k + 1) * half, :],
            NT,
            preferred_element_type=jnp.float32,
        ).astype(jnp.bfloat16)
        copy = remote(near_send.at[k], near_land.at[k], near_sem, (k,), dp=sibling)
        copy.start()
        nears.append(copy)
    fars = []
    for k in range(halves):
        slopes = own.at[pl.ds(0, chips * held_count), pl.ds(0, half)]
        slopes[...] = lax.dot_general(
            turned[core],
            w[k * half : (k + 1) * half, :],
            NT,
            preferred_element_type=jnp.float32,
        )
        nears[k].wait_recv()
        for q in range(chips):
            goal = (chip + q) % chips
            there = at(goal * held_count, held_count)
            both = slopes[there, :] + near_land[k, there, :].astype(jnp.float32)
            if q == 0:
                reduced[:, k * half : (k + 1) * half] = both
            else:
                far_send[k, q - 1] = both.astype(jnp.bfloat16)
                copy = remote(
                    far_send.at[k, q - 1],
                    far_land.at[k, q - 1],
                    far_sem,
                    (k * (chips - 1) + q - 1,),
                    dp=goal * 2 + core,
                )
                copy.start()
                fars.append(copy)

    rewards_rows = upright(rewards)
    rewards_out[...] = jnp.sum(
        place[...].astype(jnp.float32) * rewards_rows, axis=0, keepdims=True
    )
    against = -margin
    soft = jnp.maximum(against, 0.0) + jnp.log1p(jnp.exp(-jnp.abs(against)))
    loss_out[...] = jnp.sum(soft, axis=0, keepdims=True) / pairs
    head_gradient[...] = jnp.sum(direct_rows * combined[...], axis=0, keepdims=True) * gain[...]

    for k in range(halves):
        extra = None
        for q in range(1, chips):
            fars[k * (chips - 1) + q - 1].wait_recv()
            piece = far_land[k, q - 1].astype(jnp.float32)
            extra = piece if extra is None else extra + piece
        reduced[:, k * half : (k + 1) * half] += extra

    for copy in backs:
        copy.wait_recv()
    for copy in locals_[chunks:]:
        copy.wait()
    sent = infos + backs + stats + nears + fars
    for group in moves + pools + passes:
        sent = sent + group
    for copy in sent + z_copies:
        copy.wait_send()

    @pl.when(depth > 0)
    def _():
        for copy in t_copies:
            copy.wait_send()


def gradient_kernel(per, chunk_slots, target, lengths, returned, reduced, pooled, upstream, rows_out, pooled_gradient, weight_gradient):
    groups = returned.shape[0] // per
    block = groups * chunk_slots

    @pl.when(pl.program_id(0) == 0)
    def _():
        token = lax.broadcasted_iota(jnp.int32, returned.shape[1:], 0)

        def body(r, carry):
            p = target[r]
            rows_out[r] = jnp.where(token < lengths[r], returned[p], jnp.zeros_like(returned[p]))
            owner = p // per
            j = p % per
            row = j // chunk_slots * block + owner * chunk_slots + j % chunk_slots
            pooled_gradient[pl.ds(r, 1), :] = reduced[pl.ds(row, 1), :]
            return carry

        lax.fori_loop(0, rows_out.shape[0], body, 0)

    weight_gradient[...] = lax.dot_general(
        pooled[...], upstream[...], TN, preferred_element_type=jnp.float32
    )


def fused_shards(
    response_query,
    response_keys,
    prompt_cache,
    lengths,
    owners,
    pairing,
    residual,
    output_weight,
    norm_gain,
    reward_head,
):
    groups = lax.axis_size("dp")
    planes = lax.axis_size("mp")
    held_count, slot_count, width = response_query.shape
    local_heads = width // HD
    group_size = Q_HEADS // KV_HEADS
    per = held_count // groups
    count = held_count * groups
    columns = output_weight.shape[1]
    prefix = prompt_cache.shape[2]
    window = kv_window(planes, local_heads)
    chunk_slots = slots_of_chunk(groups, per)
    chunks = per // chunk_slots
    block = groups * chunk_slots
    chips = groups // 2
    span = window * HD
    packed_width = width + 2 * span
    bf16, f32 = jnp.bfloat16, jnp.float32
    vmem = pl.BlockSpec(memory_space=pltpu.VMEM)
    smem = pl.BlockSpec(memory_space=pltpu.SMEM)
    hbm = pl.BlockSpec(memory_space=pltpu.HBM)
    packed, info, target = pl.pallas_call(
        functools.partial(plan_kernel, per, chunk_slots, window),
        out_shape=(
            jax.ShapeDtypeStruct((held_count, slot_count, packed_width), bf16),
            jax.ShapeDtypeStruct((groups, 16, HD), f32),
            jax.ShapeDtypeStruct((held_count,), jnp.int32),
        ),
        in_specs=[smem, smem, hbm, hbm],
        out_specs=(vmem, vmem, smem),
        scratch_shapes=[
            pltpu.SMEM((groups,), jnp.int32),
            pltpu.VMEM((held_count, slot_count, width), bf16),
            pltpu.VMEM((2, held_count, slot_count, span), bf16),
            pltpu.SemaphoreType.DMA((3,)),
        ],
        compiler_params=pltpu.CompilerParams(vmem_limit_bytes=61 << 20),
        name="plan",
    )(owners, lengths, response_query, response_keys)
    slots = held_count * slot_count
    sub = SUB
    steps = count // sub
    halves = 2
    half = width // halves
    dma = lambda *shape: pltpu.SemaphoreType.DMA(shape)
    returned, pooled, upstream, reduced, head_gradient, rewards, loss = pl.pallas_call(
        functools.partial(
            layer_kernel, (groups, planes, per, chunk_slots, window, sub)
        ),
        out_shape=(
            jax.ShapeDtypeStruct((slots, width), bf16),
            jax.ShapeDtypeStruct((count, width), bf16),
            jax.ShapeDtypeStruct((count, columns), bf16),
            jax.ShapeDtypeStruct((held_count, width), f32),
            jax.ShapeDtypeStruct((1, columns), f32),
            jax.ShapeDtypeStruct((1, count), f32),
            jax.ShapeDtypeStruct((1, 1), f32),
        ),
        in_specs=[vmem, vmem, hbm, hbm, hbm, vmem, vmem, vmem],
        out_specs=(vmem,) * 7,
        scratch_shapes=[
            pltpu.VMEM((slots, packed_width), bf16),
            pltpu.VMEM((groups, 16, HD), f32),
            pltpu.VMEM((2, prefix, span), bf16),
            pltpu.VMEM((width, columns), bf16),
            pltpu.VMEM((count, columns), bf16),
            pltpu.VMEM((count, count), bf16),
            pltpu.VMEM((count // 2, count), f32),
            pltpu.VMEM((groups * block, groups * block), bf16),
            pltpu.VMEM((count, columns), f32),
            pltpu.VMEM((slots, width), bf16),
            pltpu.VMEM((count, columns), f32),
            pltpu.VMEM((count, columns), bf16),
            pltpu.VMEM((2, count, columns), bf16),
            pltpu.VMEM((count, columns), bf16),
            pltpu.VMEM((count, columns), f32),
            pltpu.VMEM((8, HD), f32),
            pltpu.VMEM((groups, 8, HD), f32),
            pltpu.VMEM((2, chips * held_count, columns), bf16),
            pltpu.VMEM((halves, chips * held_count, half), bf16),
            pltpu.VMEM((halves, chips * held_count, half), bf16),
            pltpu.VMEM((halves, chips - 1, held_count, half), bf16),
            pltpu.VMEM((halves, chips - 1, held_count, half), bf16),
            dma(4),
            dma(2, groups - 1),
            dma(2, chunks * (groups - 1)),
            dma(2 * chunks),
            dma(2, chunks * chips),
            dma(2, chunks * (chips - 1)),
            dma(2, chunks * (groups - 1)),
            dma(2, 2, steps),
            dma(2, steps),
            dma(2, groups - 1),
            dma(2, halves),
            dma(2, halves * (chips - 1)),
        ],
        compiler_params=pltpu.CompilerParams(
            collective_id=0, has_side_effects=True, vmem_limit_bytes=44 << 20
        ),
        name="layer",
    )(
        packed.reshape(slots, packed_width),
        info,
        prompt_cache,
        output_weight,
        residual,
        norm_gain[None],
        reward_head[None],
        pairing[None],
    )
    tile = 512
    attention_rows, pooled_gradient, weight_gradient = pl.pallas_call(
        functools.partial(gradient_kernel, per, chunk_slots),
        out_shape=(
            jax.ShapeDtypeStruct(response_query.shape, bf16),
            jax.ShapeDtypeStruct((held_count, width), f32),
            jax.ShapeDtypeStruct((width, columns), f32),
        ),
        grid=(width // tile,),
        in_specs=[
            smem,
            smem,
            pl.BlockSpec((held_count, slot_count, width), lambda i: (0, 0, 0)),
            pl.BlockSpec((held_count, width), lambda i: (0, 0)),
            pl.BlockSpec((count, tile), lambda i: (0, i)),
            pl.BlockSpec((count, columns), lambda i: (0, 0)),
        ],
        out_specs=(
            pl.BlockSpec((held_count, slot_count, width), lambda i: (0, 0, 0)),
            pl.BlockSpec((held_count, width), lambda i: (0, 0)),
            pl.BlockSpec((tile, columns), lambda i: (i, 0)),
        ),
        compiler_params=pltpu.CompilerParams(vmem_limit_bytes=32 << 20),
        name="gradient",
    )(
        target,
        lengths,
        returned.reshape(held_count, slot_count, width),
        reduced,
        pooled,
        upstream,
    )
    return (
        attention_rows,
        rewards[0],
        loss[0, 0],
        weight_gradient,
        head_gradient[0],
        pooled_gradient,
    )


SUB = 32


def kv_window(planes, local_heads):
    group_size = Q_HEADS // KV_HEADS
    return max(
        (m * local_heads + local_heads - 1) // group_size - m * local_heads // group_size + 1
        for m in range(planes)
    )


def slots_of_chunk(groups, per):
    for slots in range(1, per + 1):
        if per % slots == 0 and slots * groups % 16 == 0:
            return slots
    return 0


def fits(shape, responses):
    groups, planes = shape["dp"], shape["mp"]
    held = responses // groups
    if held % groups or groups % 2 or planes % 2:
        return False
    slots = slots_of_chunk(groups, held // groups)
    return bool(slots) and slots * groups * 8 == HD and responses % HD == 0 and responses <= 3 * HD


def shards(*args):
    held = args[0].shape[0]
    groups = lax.axis_size("dp")
    sizes = {"dp": groups, "mp": lax.axis_size("mp")}
    if fits(sizes, held * groups):
        return fused_shards(*args)
    return stepwise_shards(*args)


def solution(mesh):
    placed = (
        P("dp", None, "mp"),
        P(None, "dp", None, None),
        P(None, "dp", None, None),
        P("dp"),
        P("dp"),
        P(),
        P(None, "dp"),
        P("mp", "dp"),
        P("dp"),
        P("dp"),
    )
    return jax.shard_map(
        shards,
        mesh=mesh,
        in_specs=placed,
        out_specs=(P("dp", None, "mp"), P(), P(), P("mp", "dp"), P("dp"), P("dp", "mp")),
        check_vma=False,
    )
```

```python
import functools
import math

import jax
import jax.numpy as jnp
from jax import lax
from jax.experimental import pallas as pl
from jax.experimental.pallas import tpu as pltpu
from jax.sharding import PartitionSpec as P

D = 8192
HD = 128
Q_HEADS = 48
KV_HEADS = 6


EPSILON = 1e-05


def bradley_terry(rewards, pairing):
    count = rewards.shape[0]
    chosen = pairing[0::2, None] == jnp.arange(count)[None, :]
    rejected = pairing[1::2, None] == jnp.arange(count)[None, :]
    sign = chosen.astype(jnp.float32) - rejected.astype(jnp.float32)
    margin = jnp.sum(sign * rewards[None, :], axis=1)
    loss_value = jnp.mean(jax.nn.softplus(-margin))
    slope = -jax.nn.sigmoid(-margin) / margin.shape[0]
    reward_slope = jnp.sum(sign * slope[:, None], axis=0)
    return (loss_value, reward_slope)


def pack_kernel(window, meta, query, keys, out, late):
    slots = out.shape[0]
    rest = late.shape[2]
    width = query.shape[2] - rest
    span = window * HD
    first = pl.multiple_of(meta[2 * slots] * HD, HD)

    def body(p, carry):
        r = meta[p]
        out[p, :, pl.ds(0, width)] = query[r, :, pl.ds(0, width)]
        late[p] = query[r, :, pl.ds(width, rest)]
        out[p, :, pl.ds(width, span)] = keys[0, r, :, pl.ds(first, span)]
        out[p, :, pl.ds(width + span, span)] = keys[1, r, :, pl.ds(first, span)]
        length = meta[slots + p].astype(jnp.float32)
        place = r.astype(jnp.float32)
        lane = lax.broadcasted_iota(jnp.int32, (out.shape[1], HD), 1)
        out[p, :, pl.ds(width + 2 * span, HD)] = jnp.where(lane < HD // 2, length, place).astype(
            jnp.bfloat16
        )
        return carry

    lax.fori_loop(0, slots, body, 0)


def attention_kernel(slot_count, placed, meta, query, own_k, own_v, lens, cache, out, pooled):
    rows = query.shape[0]
    head = pl.program_id(0)
    chunk = 128
    blocks = chunk // slot_count
    scale = math.log2(math.e) / math.sqrt(HD)
    contract = (((1,), (1,)), ((), ()))
    row = lax.broadcasted_iota(jnp.int32, (chunk, chunk), 0)
    col = lax.broadcasted_iota(jnp.int32, (chunk, chunk), 1)
    t = row % slot_count
    s = col % slot_count
    causal = (row // slot_count == col // slot_count) & (s <= t)
    s_float = s.astype(jnp.float32)
    t_float = t.astype(jnp.float32)
    gather = lax.broadcasted_iota(jnp.int32, (blocks, chunk), 0)
    member = lax.broadcasted_iota(jnp.int32, (blocks, chunk), 1)
    gather = jnp.where(gather == member // slot_count, 1.0, 0.0).astype(jnp.bfloat16)
    for start in range(0, rows, chunk):
        here = pl.ds(start, chunk)
        q = query[here, :]
        length = jnp.broadcast_to(lens[here, :].astype(jnp.float32)[:, 0:1], (chunk, chunk))
        far = lax.dot_general(q, cache[0, 0], contract, preferred_element_type=jnp.float32)
        near = lax.dot_general(q, own_k[here, :], contract, preferred_element_type=jnp.float32)
        near = jnp.where(causal & (s_float < length), near, -jnp.inf)
        top = jnp.maximum(
            jnp.max(far, axis=1, keepdims=True), jnp.max(near, axis=1, keepdims=True)
        )
        far = jnp.exp2((far - top) * scale)
        near = jnp.exp2((near - top) * scale)
        total = jnp.sum(far, axis=1, keepdims=True) + jnp.sum(near, axis=1, keepdims=True)
        value = jnp.dot(far.astype(jnp.bfloat16), cache[1, 0], preferred_element_type=jnp.float32)
        value += jnp.dot(
            near.astype(jnp.bfloat16), own_v[here, :], preferred_element_type=jnp.float32
        )
        value = jnp.where(t_float < length, value / total, 0.0)
        out[here, :] = value.astype(jnp.bfloat16)
        last = jnp.where(t_float == length - 1.0, value, 0.0)
        last = jnp.dot(gather, last.astype(jnp.bfloat16), preferred_element_type=jnp.float32)
        there = pl.ds(start // slot_count, blocks)
        pooled[there, pl.ds(pl.multiple_of(head * HD, HD), HD)] = last.astype(jnp.bfloat16)

        if placed:

            @pl.when(head == 0)
            def _():
                place = lens[here, :].astype(jnp.float32).reshape(blocks, slot_count, HD)
                pooled[there, pl.ds(pooled.shape[1] - HD, HD)] = jnp.max(place, axis=1).astype(
                    jnp.bfloat16
                )


def unpack_kernel(meta, returned, out):
    def body(r, carry):
        out[r] = returned[meta[r]]
        return carry

    lax.fori_loop(0, out.shape[0], body, 0)


def stepwise_shards(
    response_query,
    response_keys,
    prompt_cache,
    lengths,
    owners,
    pairing,
    residual,
    output_weight,
    norm_gain,
    reward_head,
):
    groups = lax.axis_size("dp")
    planes = lax.axis_size("mp")
    model_rank = lax.axis_index("mp")
    held_count, slot_count, head_width = response_query.shape
    local_heads = head_width // HD
    group_size = Q_HEADS // KV_HEADS
    per_owner = (held_count + groups - 1) // groups
    capacity = groups * per_owner
    window = max(
        (m * local_heads + local_heads - 1) // group_size - m * local_heads // group_size + 1
        for m in range(planes)
    )
    first_head = jnp.minimum(model_rank * local_heads // group_size, KV_HEADS - window)
    head_kv = (model_rank * local_heads + jnp.arange(local_heads)) // group_size
    positions = jnp.arange(held_count)
    earlier = (owners[None, :] == owners[:, None]) & (positions[None, :] < positions[:, None])
    target = (owners * per_owner + jnp.sum(earlier, axis=1)).astype(jnp.int32)
    sent_from = (target[None, :] == jnp.arange(capacity)[:, None]).astype(jnp.int32)
    source = jnp.sum(sent_from * positions[None, :], axis=1)
    slot_length = jnp.sum(sent_from * lengths[None, :], axis=1)
    params = pltpu.CompilerParams(vmem_limit_bytes=40 * 1024 * 1024)
    vmem = pl.BlockSpec(memory_space=pltpu.VMEM)
    smem = pl.BlockSpec(memory_space=pltpu.SMEM)
    early = local_heads - local_heads // 2
    late_width = local_heads // 2 * HD
    packed_width = early * HD + (2 * window + 1) * HD
    packed, late = pl.pallas_call(
        functools.partial(pack_kernel, window),
        out_shape=(
            jax.ShapeDtypeStruct((capacity, slot_count, packed_width), jnp.bfloat16),
            jax.ShapeDtypeStruct((capacity, slot_count, late_width), jnp.bfloat16),
        ),
        in_specs=[smem, vmem, vmem],
        out_specs=(vmem, vmem),
        compiler_params=params,
        name="pack",
    )(
        jnp.concatenate([source, slot_length, first_head[None]]).astype(jnp.int32),
        response_query,
        response_keys,
    )
    packed = packed.reshape(groups, per_owner, slot_count, packed_width)
    arrived = lax.all_to_all(packed, "dp", split_axis=0, concat_axis=0, tiled=True)
    late = late.reshape(groups, per_owner, slot_count, late_width)
    late = lax.all_to_all(late, "dp", split_axis=0, concat_axis=0, tiled=True)
    rows = capacity * slot_count
    late = late.reshape(rows, late_width)
    arrived = arrived.reshape(rows, packed_width)
    block = (rows, HD)

    def attend(query, head_base, heads, placed):
        pooled_width = (heads + placed) * HD
        at = lambda meta, h: meta[local_heads + head_base + h]
        return pl.pallas_call(
            functools.partial(attention_kernel, slot_count, placed),
            out_shape=(
                jax.ShapeDtypeStruct((rows, heads * HD), jnp.bfloat16),
                jax.ShapeDtypeStruct((capacity, pooled_width), jnp.bfloat16),
            ),
            grid_spec=pltpu.PrefetchScalarGridSpec(
                num_scalar_prefetch=1,
                grid=(heads,),
                in_specs=[
                    pl.BlockSpec(block, lambda h, meta: (0, h)),
                    pl.BlockSpec(block, lambda h, meta: (0, early + at(meta, h))),
                    pl.BlockSpec(block, lambda h, meta: (0, early + window + at(meta, h))),
                    pl.BlockSpec(block, lambda h, meta: (0, early + 2 * window)),
                    pl.BlockSpec(
                        (2, 1, prompt_cache.shape[2], HD),
                        lambda h, meta: (0, 0, 0, meta[head_base + h]),
                    ),
                ],
                out_specs=(
                    pl.BlockSpec(block, lambda h, meta: (0, h)),
                    pl.BlockSpec((capacity, pooled_width), lambda h, meta: (0, 0)),
                ),
            ),
            compiler_params=params,
            cost_estimate=pl.CostEstimate(
                flops=4 * rows * heads * HD * prompt_cache.shape[2],
                bytes_accessed=8 * rows * heads * HD,
                transcendentals=rows * heads * prompt_cache.shape[2],
            ),
            name="attention_early" if placed else "attention_late",
        )(
            jnp.concatenate([head_kv, head_kv - first_head]).astype(jnp.int32),
            query,
            arrived,
            arrived,
            arrived,
            prompt_cache,
        )

    def share_rows(own):
        copies = jnp.broadcast_to(own[None], (groups,) + own.shape)
        copies = lax.all_to_all(copies, "dp", split_axis=0, concat_axis=0, tiled=True)
        return copies.reshape(groups * own.shape[0], own.shape[1])

    attended_early, pooled_early = attend(arrived, 0, early, True)
    pooled_slots = share_rows(pooled_early)
    attended_late, pooled_late = attend(late, early, local_heads - early, False)
    pooled_late = share_rows(pooled_late)
    attended = jnp.concatenate([attended_early, attended_late], axis=1)
    result = attended.reshape(groups, per_owner, slot_count, head_width)
    returned = lax.all_to_all(result, "dp", split_axis=0, concat_axis=0, tiled=True)
    attention_rows = pl.pallas_call(
        unpack_kernel,
        out_shape=jax.ShapeDtypeStruct(response_query.shape, jnp.bfloat16),
        in_specs=[smem, vmem],
        out_specs=vmem,
        compiler_params=params,
        name="unpack",
    )(target, returned.reshape(capacity, slot_count, head_width))
    count = held_count * groups
    sender = jnp.arange(capacity * groups) % capacity // per_owner
    place = pooled_slots[:, early * HD + HD - 1].astype(jnp.int32)
    live = pooled_slots[:, early * HD] > 0
    response = jnp.where(live, sender * held_count + place, count)
    order = (jnp.arange(count)[:, None] == response[None, :]).astype(jnp.bfloat16)
    pooled_all = jnp.concatenate(
        [
            jnp.dot(order, slots, preferred_element_type=jnp.float32).astype(jnp.bfloat16)
            for slots in (pooled_slots[:, : early * HD], pooled_late)
        ],
        axis=1,
    )
    share = count // planes
    partial_mix = jnp.dot(pooled_all, output_weight, preferred_element_type=jnp.float32)
    columns = output_weight.shape[1]
    scaled_head = norm_gain * reward_head
    shares = lax.all_to_all(
        partial_mix.astype(jnp.bfloat16).reshape(planes, share, columns),
        "mp",
        split_axis=0,
        concat_axis=0,
        tiled=True,
    )
    part = jnp.sum(shares.astype(jnp.float32), axis=0) + lax.dynamic_slice_in_dim(
        residual, model_rank * share, share, 0
    ).astype(jnp.float32)
    combined = lax.all_gather(part.astype(jnp.bfloat16), "mp", axis=0, tiled=True).astype(
        jnp.float32
    )
    square_sum = jnp.sum(combined * combined, axis=1)
    signal = jnp.sum(combined * scaled_head[None, :], axis=1)
    square_sum, signal = lax.psum((square_sum, signal), "dp")
    inverse = lax.rsqrt(square_sum / D + EPSILON)
    rewards = inverse * signal
    pair_loss, reward_slope = bradley_terry(rewards, pairing)
    direct_term = reward_slope * inverse
    norm_term = reward_slope * inverse * inverse * inverse * signal / D
    upstream = direct_term[:, None] * scaled_head[None, :] - norm_term[:, None] * combined
    head_gradient = jnp.sum(direct_term[:, None] * combined * norm_gain[None, :], axis=0)
    upstream_half = upstream.astype(jnp.bfloat16)
    slope_part = lax.dot_general(
        upstream_half,
        output_weight,
        (((1,), (1,)), ((), ())),
        preferred_element_type=jnp.float32,
    ).astype(jnp.bfloat16)
    slope_parts = lax.all_to_all(
        slope_part.reshape(groups, held_count, head_width),
        "dp",
        split_axis=0,
        concat_axis=0,
        tiled=True,
    )
    weight_gradient = lax.dot_general(
        pooled_all, upstream_half, (((0,), (0,)), ((), ())), preferred_element_type=jnp.float32
    )
    pooled_gradient = jnp.sum(slope_parts.astype(jnp.float32), axis=0)
    return (attention_rows, rewards, pair_loss, weight_gradient, head_gradient, pooled_gradient)


MESH = pl.DeviceIdType.MESH
NT = (((1,), (1,)), ((), ()))
TN = (((0,), (0,)), ((), ()))


def plan_kernel(per, chunk_slots, window, owners, lengths, query, keys, packed, info, target, count, got, held, sems):
    me = lax.axis_index("dp")
    groups = count.shape[0]
    held_count = query.shape[0]
    width = query.shape[2]
    span = window * HD
    first = jnp.minimum(
        lax.axis_index("mp") * (width // HD) // (Q_HEADS // KV_HEADS), KV_HEADS - window
    )
    columns = pl.ds(pl.multiple_of(first * HD, HD), span)
    loads = [
        pltpu.make_async_copy(query, got, sems.at[0]),
        pltpu.make_async_copy(keys.at[0, :, :, columns], held.at[0], sems.at[1]),
        pltpu.make_async_copy(keys.at[1, :, :, columns], held.at[1], sems.at[2]),
    ]
    for load in loads:
        load.start()
    for owner in range(groups):
        count[owner] = 0
    spot = lax.broadcasted_iota(jnp.int32, (8, HD), 0) * HD + lax.broadcasted_iota(
        jnp.int32, (8, HD), 1
    )
    block = groups * chunk_slots

    def place(r, rows):
        owner = owners[r]
        j = count[owner]
        count[owner] = j + 1
        target[r] = owner * per + j
        info[owner, pl.ds(j, 1), :] = jnp.full((1, HD), lengths[r], jnp.int32).astype(jnp.float32)
        row = (
            j // chunk_slots * (groups * block) + owner * block + j % chunk_slots * groups + me
        )
        return jnp.where(spot == me * held_count + r, row, rows)

    rows = lax.fori_loop(0, held_count, place, jnp.zeros((8, HD), jnp.int32))
    for owner in range(groups):
        info[owner, pl.ds(8, 8), :] = rows.astype(jnp.float32)
    for load in loads:
        load.wait()

    def move(r, carry):
        p = target[r]
        packed[p, :, pl.ds(0, width)] = got[r]
        packed[p, :, pl.ds(width, span)] = held[0, r]
        packed[p, :, pl.ds(width + span, span)] = held[1, r]
        return carry

    lax.fori_loop(0, held_count, move, 0)


def layer_kernel(
    sizes,
    packed,
    info,
    cache,
    weight,
    residual,
    gain,
    head,
    pairing,
    returned,
    pooled,
    upstream,
    reduced,
    head_gradient,
    rewards_out,
    loss_out,
    land,
    info_land,
    kv,
    w,
    res,
    place,
    sign,
    turn,
    shifted,
    attended,
    own,
    z_send,
    z_land,
    z_total,
    combined,
    stat,
    stat_land,
    turned,
    near_send,
    near_land,
    far_send,
    far_land,
    load_sem,
    info_sem,
    move_sem,
    local_sem,
    pool_sem,
    pass_sem,
    back_sem,
    z_sem,
    t_sem,
    stat_sem,
    near_sem,
    far_sem,
):
    groups, planes, per, chunk_slots, window, sub = sizes
    held_count = reduced.shape[0]
    me = lax.axis_index("dp")
    rank = lax.axis_index("mp")
    chips = groups // 2
    chip = me // 2
    core = me % 2
    sibling = chip * 2 + 1 - core
    chunks = per // chunk_slots
    block = groups * chunk_slots
    unit = chunk_slots * 8
    rows = block * 8
    mixed = groups * block
    width = attended.shape[1]
    local_heads = width // HD
    group_size = Q_HEADS // KV_HEADS
    stack = math.gcd(local_heads, group_size)
    span = window * HD
    count = pooled.shape[0]
    first = jnp.minimum(rank * local_heads // group_size, KV_HEADS - window)
    columns = pl.ds(pl.multiple_of(first * HD, HD), span)

    def remote(src, dst, sem, index, **where):
        return pltpu.make_async_remote_copy(
            src_ref=src,
            dst_ref=dst,
            send_sem=sem.at[(0,) + index],
            recv_sem=sem.at[(1,) + index],
            device_id=where,
            device_id_type=MESH,
        )

    def at(start, size):
        return pl.ds(pl.multiple_of(start, size), size)

    loads = [
        pltpu.make_async_copy(cache.at[0, 0, :, columns], kv.at[0], load_sem.at[0]),
        pltpu.make_async_copy(cache.at[1, 0, :, columns], kv.at[1], load_sem.at[1]),
        pltpu.make_async_copy(residual, res, load_sem.at[2]),
        pltpu.make_async_copy(weight, w, load_sem.at[3]),
    ]
    for load in loads:
        load.start()

    barrier = pltpu.get_barrier_semaphore()
    for d in range(1, groups):
        pl.semaphore_signal(
            barrier, inc=1, device_id={"dp": (me + d) % groups}, device_id_type=MESH
        )
    for d in range(1, planes):
        pl.semaphore_signal(
            barrier, inc=1, device_id={"mp": (rank + d) % planes}, device_id_type=MESH
        )
    pl.semaphore_wait(barrier, groups + planes - 2)

    infos = []
    for d in range(1, groups):
        peer = (me + d) % groups
        copy = remote(info.at[peer], info_land.at[me], info_sem, (d - 1,), dp=peer)
        copy.start()
        infos.append(copy)
    moves = []
    locals_ = []

    def dispatch(c):
        moves.append([])
        for d in range(1, groups):
            peer = (me + d) % groups
            copy = remote(
                packed.at[at((peer * chunks + c) * unit, unit), :],
                land.at[at((c * groups + me) * unit, unit), :],
                move_sem,
                (c * (groups - 1) + d - 1,),
                dp=peer,
            )
            copy.start()
            moves[c].append(copy)
        copy = pltpu.make_async_copy(
            packed.at[at((me * chunks + c) * unit, unit), :],
            land.at[at((c * groups + me) * unit, unit), :],
            local_sem.at[c],
        )
        copy.start()
        locals_.append(copy)

    dispatch(0)

    info_land[me] = info[me]
    for copy in infos:
        copy.wait_recv()
    row_of = info_land[0, pl.ds(8, 8), :]
    for g in range(1, groups):
        row_of = row_of + info_land[g, pl.ds(8, 8), :]
    row_of = row_of.astype(jnp.int32)
    row_at = lax.broadcasted_iota(jnp.int32, (count, HD), 0)
    for a in range(count // HD):
        place[:, a * HD : (a + 1) * HD] = jnp.where(
            row_at == row_of[a : a + 1, :], 1.0, 0.0
        ).astype(jnp.bfloat16)
    asked = jnp.where(
        lax.broadcasted_iota(jnp.int32, (count, count), 0) == pairing[...], 1.0, 0.0
    ).astype(jnp.bfloat16)
    pair = lax.broadcasted_iota(jnp.int32, (count // 2, count), 0) * 2
    entry = lax.broadcasted_iota(jnp.int32, (count // 2, count), 1)
    side = jnp.where(entry == pair, 1.0, jnp.where(entry == pair + 1, -1.0, 0.0))
    chosen = lax.dot_general(
        side.astype(jnp.bfloat16), asked, NT, preferred_element_type=jnp.float32
    )
    sign[...] = lax.dot_general(
        chosen.astype(jnp.bfloat16), place[...], NT, preferred_element_type=jnp.float32
    )
    loads[2].wait()
    shifted[...] = jnp.dot(place[...], res[...], preferred_element_type=jnp.float32)

    new = lax.broadcasted_iota(jnp.int32, (mixed, mixed), 0)
    old = lax.broadcasted_iota(jnp.int32, (mixed, mixed), 1)
    old_at = new % block * groups + new // block % chips * 2 + new // (block * chips)
    turn[...] = jnp.where(old == old_at, 1.0, 0.0).astype(jnp.bfloat16)

    for copy in moves[0]:
        copy.wait_send()
    if chunks > 1:
        dispatch(1)
    scale = math.log2(math.e) / math.sqrt(HD)
    tall = stack * rows

    def attend(c):
        here = pl.ds(c * rows, rows)
        row = lax.broadcasted_iota(jnp.int32, (tall, rows), 0) % rows
        col = lax.broadcasted_iota(jnp.int32, (tall, rows), 1)
        causal = (row // 8 == col // 8) & (col <= row)
        for s in range(local_heads // stack):
            part = (rank * local_heads + stack * s) // group_size - first
            query = jnp.concatenate(
                [
                    land[here, h * HD : (h + 1) * HD]
                    for h in range(s * stack, (s + 1) * stack)
                ],
                axis=0,
            )
            own_k = land[here, pl.ds(pl.multiple_of(width + part * HD, HD), HD)]
            own_v = land[here, pl.ds(pl.multiple_of(width + span + part * HD, HD), HD)]
            key = kv[0, :, pl.ds(pl.multiple_of(part * HD, HD), HD)]
            value = kv[1, :, pl.ds(pl.multiple_of(part * HD, HD), HD)]
            far = lax.dot_general(query, key, NT, preferred_element_type=jnp.float32)
            near = lax.dot_general(query, own_k, NT, preferred_element_type=jnp.float32)
            near = jnp.where(causal, near, -1e30)
            top = jnp.maximum(
                jnp.max(far, axis=1, keepdims=True), jnp.max(near, axis=1, keepdims=True)
            )
            far = jnp.exp2((far - top) * scale).astype(jnp.bfloat16)
            near = jnp.exp2((near - top) * scale).astype(jnp.bfloat16)
            ones = lambda v: jnp.concatenate([v, jnp.ones_like(v)], axis=1)
            both = jnp.dot(far, ones(value), preferred_element_type=jnp.float32)
            both += jnp.dot(near, ones(own_v), preferred_element_type=jnp.float32)
            out = (both[:, :HD] / both[:, HD:]).astype(jnp.bfloat16)
            for h in range(stack):
                attended[here, (s * stack + h) * HD : (s * stack + h + 1) * HD] = out[
                    h * rows : (h + 1) * rows
                ]

    pools = []
    passes = []

    def share(c):
        slots = [
            jnp.concatenate(
                [info_land[g, pl.ds(c * chunk_slots + k, 1), :] for g in range(groups)], axis=0
            )
            for k in range(chunk_slots)
        ]
        length = jnp.concatenate(slots, axis=0).astype(jnp.int32)
        i = lax.broadcasted_iota(jnp.int32, (block, HD), 0)
        col = lax.broadcasted_iota(jnp.int32, (block, HD), 1)
        start = (i % groups * chunk_slots + i // groups) * 8 - 1
        pick = jnp.where(col == start + length, 1.0, 0.0).astype(jnp.bfloat16)
        last = jnp.dot(
            pick, attended[pl.ds(c * rows, rows), :], preferred_element_type=jnp.float32
        )
        mine = at(c * mixed + me * block, block)
        pooled[mine, :] = last.astype(jnp.bfloat16)
        sent = []
        for q in range(1, chips):
            sent.append(
                remote(
                    pooled.at[mine, :],
                    pooled.at[mine, :],
                    pool_sem,
                    (c * chips + q,),
                    dp=(chip + q) % chips * 2 + core,
                )
            )
        sent.append(
            remote(
                pooled.at[mine, :], pooled.at[mine, :], pool_sem, (c * chips,), dp=sibling
            )
        )
        for copy in sent:
            copy.start()
        pools.append(sent)

    def pass_on(c):
        sent = []
        for q in range(1, chips):
            pools[c][q - 1].wait_recv()
            source = (chip + chips - q) % chips * 2 + core
            there = at(c * mixed + source * block, block)
            copy = remote(
                pooled.at[there, :],
                pooled.at[there, :],
                pass_sem,
                (c * (chips - 1) + q - 1,),
                dp=sibling,
            )
            copy.start()
            sent.append(copy)
        passes.append(sent)

    depth = jnp.minimum(rank, planes - 1 - rank)
    centre = planes // 2 - 1
    is_centre = depth == centre
    low = rank < planes // 2
    inward = jnp.where(low, rank + 1, rank - 1)
    outward = jnp.where(low, rank - 1, rank + 1)
    outward = jnp.where(depth == 0, inward, outward)
    slot = jnp.where(is_centre, 1, 0)
    steps = mixed // sub
    z_copies = [
        remote(
            z_send.at[pl.ds(n * sub, sub), :],
            z_land.at[slot, pl.ds(n * sub, sub), :],
            z_sem,
            (slot, n),
            mp=inward,
        )
        for n in range(chunks * steps)
    ]
    z_waits = [
        [
            remote(
                z_send.at[pl.ds(n * sub, sub), :],
                z_land.at[k, pl.ds(n * sub, sub), :],
                z_sem,
                (k, n),
                mp=inward,
            )
            for n in range(chunks * steps)
        ]
        for k in range(2)
    ]
    t_copies = [
        remote(
            z_total.at[pl.ds(n * sub, sub), :],
            z_total.at[pl.ds(n * sub, sub), :],
            t_sem,
            (n,),
            mp=outward,
        )
        for n in range(chunks * steps)
    ]

    def mix(c):
        for copy in passes[c]:
            copy.wait_recv()
        pools[c][-1].wait_recv()
        if c == 0:
            loads[3].wait()
        here = pl.ds(c * mixed, mixed)
        product = jnp.dot(pooled[here, :], w[...], preferred_element_type=jnp.float32)
        own[here, :] = product
        z_send[here, :] = product.astype(jnp.bfloat16)

        @pl.when(depth == 0)
        def _():
            for n in range(c * steps, (c + 1) * steps):
                z_copies[n].start()

    def inner(n):
        here = pl.ds(n * sub, sub)

        @pl.when(depth > 0)
        def _():
            z_waits[0][n].wait_recv()
            z_send[here, :] = (own[here, :] + z_land[0, here, :].astype(jnp.float32)).astype(
                jnp.bfloat16
            )
            z_copies[n].start()

    scaled_head = gain[...] * head[...]

    def finish(n):
        here = pl.ds(n * sub, sub)

        @pl.when(is_centre)
        def _():
            z_waits[1][n].wait_recv()
            z_total[here, :] = (
                z_send[here, :].astype(jnp.float32) + z_land[1, here, :].astype(jnp.float32)
            ).astype(jnp.bfloat16)

        @pl.when(depth < centre)
        def _():
            t_copies[n].wait_recv()

        @pl.when(depth > 0)
        def _():
            t_copies[n].start()

        whole = z_total[here, :].astype(jnp.float32) + shifted[here, :]
        combined[here, :] = whole
        square = jnp.sum(whole * whole, axis=1, keepdims=True)
        signal = jnp.sum(whole * scaled_head, axis=1, keepdims=True)
        lane = lax.broadcasted_iota(jnp.int32, (sub, HD), 1)
        this = lax.broadcasted_iota(jnp.int32, (sub, HD), 0) + n * sub % HD
        line = n * sub // HD
        for k, column in enumerate((square, signal)):
            spread = jnp.sum(jnp.where(lane == this, column, 0.0), axis=0, keepdims=True)
            there = pl.ds(k * (count // HD) + line, 1)
            if n * sub % HD == 0:
                stat[there, :] = spread
            else:
                stat[there, :] += spread

    backs = []

    def give_back(c):
        for d in range(1, groups):
            peer = (me + d) % groups
            copy = remote(
                attended.at[at((c * groups + peer) * unit, unit), :],
                returned.at[at((me * chunks + c) * unit, unit), :],
                back_sem,
                (c * (groups - 1) + d - 1,),
                dp=peer,
            )
            copy.start()
            backs.append(copy)
        copy = pltpu.make_async_copy(
            attended.at[at((c * groups + me) * unit, unit), :],
            returned.at[at((me * chunks + c) * unit, unit), :],
            local_sem.at[chunks + c],
        )
        copy.start()
        locals_.append(copy)

    for c in range(chunks):
        for copy in moves[c]:
            copy.wait_recv()
        locals_[c].wait()
        if 0 < c < chunks - 1:
            dispatch(c + 1)
        if c == 0:
            loads[0].wait()
            loads[1].wait()
        attend(c)
        share(c)
        if c == chunks - 1:
            for n in range((chunks - 2) * steps):
                inner(n)
        if c > 0:
            pass_on(c - 1)
            mix(c - 1)
    taken = (chunks - 2) * steps
    pass_on(chunks - 1)
    for c in range(chunks):
        give_back(c)
    mix(chunks - 1)
    total = chunks * steps
    done = 0
    for n in range(taken, total):
        inner(n)
        while done < n - 1 + (n == total - 1):
            finish(done)
            done += 1
    while done < total:
        finish(done)
        done += 1

    lines = count // HD
    stat[pl.ds(2 * lines, 8 - 2 * lines), :] = jnp.zeros((8 - 2 * lines, HD), jnp.float32)
    stats = []
    for d in range(1, groups):
        copy = remote(stat, stat_land.at[me], stat_sem, (d - 1,), dp=(me + d) % groups)
        copy.start()
        stats.append(copy)
    stat_land[me] = stat[...]
    for copy in stats:
        copy.wait_recv()
    sums = stat_land[0]
    for g in range(1, groups):
        sums = sums + stat_land[g]
    square_sum = jnp.concatenate([sums[a : a + 1] for a in range(lines)], axis=1)
    signal = jnp.concatenate([sums[lines + a : lines + a + 1] for a in range(lines)], axis=1)
    inverse = lax.rsqrt(square_sum / D + EPSILON)
    rewards = inverse * signal
    margin = jnp.sum(sign[...] * rewards, axis=1, keepdims=True)
    pairs = count // 2
    slope = -jax.nn.sigmoid(-margin) / pairs
    reward_slope = jnp.sum(sign[...] * slope, axis=0, keepdims=True)
    direct = reward_slope * inverse
    norm = direct * inverse * inverse * signal / D
    eye = lax.broadcasted_iota(jnp.int32, (HD, HD), 0) == lax.broadcasted_iota(
        jnp.int32, (HD, HD), 1
    )

    def upright(line):
        return jnp.concatenate(
            [
                jnp.sum(
                    jnp.where(eye, line[:, a * HD : (a + 1) * HD], 0.0), axis=1, keepdims=True
                )
                for a in range(lines)
            ],
            axis=0,
        )

    direct_rows = upright(direct)
    norm_rows = upright(norm)
    for c in range(chunks):
        here = pl.ds(c * mixed, mixed)
        part = (
            direct_rows[c * mixed : (c + 1) * mixed] * scaled_head
            - norm_rows[c * mixed : (c + 1) * mixed] * combined[here, :]
        ).astype(jnp.bfloat16)
        upstream[here, :] = part
        part = jnp.dot(turn[...], part, preferred_element_type=jnp.float32).astype(jnp.bfloat16)
        for k in range(groups):
            turned[k // chips, pl.ds(k % chips * held_count + c * block, block), :] = part[
                k * block : (k + 1) * block
            ]
    halves = near_send.shape[0]
    half = width // halves
    nears = []
    for k in range(halves):
        near_send[k] = lax.dot_general(
            turned[1 - core],
            w[k * half : (k + 1) * half, :],
            NT,
            preferred_element_type=jnp.float32,
        ).astype(jnp.bfloat16)
        copy = remote(near_send.at[k], near_land.at[k], near_sem, (k,), dp=sibling)
        copy.start()
        nears.append(copy)
    fars = []
    for k in range(halves):
        slopes = own.at[pl.ds(0, chips * held_count), pl.ds(0, half)]
        slopes[...] = lax.dot_general(
            turned[core],
            w[k * half : (k + 1) * half, :],
            NT,
            preferred_element_type=jnp.float32,
        )
        nears[k].wait_recv()
        for q in range(chips):
            goal = (chip + q) % chips
            there = at(goal * held_count, held_count)
            both = slopes[there, :] + near_land[k, there, :].astype(jnp.float32)
            if q == 0:
                reduced[:, k * half : (k + 1) * half] = both
            else:
                far_send[k, q - 1] = both.astype(jnp.bfloat16)
                copy = remote(
                    far_send.at[k, q - 1],
                    far_land.at[k, q - 1],
                    far_sem,
                    (k * (chips - 1) + q - 1,),
                    dp=goal * 2 + core,
                )
                copy.start()
                fars.append(copy)

    rewards_rows = upright(rewards)
    rewards_out[...] = jnp.sum(
        place[...].astype(jnp.float32) * rewards_rows, axis=0, keepdims=True
    )
    against = -margin
    soft = jnp.maximum(against, 0.0) + jnp.log1p(jnp.exp(-jnp.abs(against)))
    loss_out[...] = jnp.sum(soft, axis=0, keepdims=True) / pairs
    head_gradient[...] = jnp.sum(direct_rows * combined[...], axis=0, keepdims=True) * gain[...]

    for k in range(halves):
        extra = None
        for q in range(1, chips):
            fars[k * (chips - 1) + q - 1].wait_recv()
            piece = far_land[k, q - 1].astype(jnp.float32)
            extra = piece if extra is None else extra + piece
        reduced[:, k * half : (k + 1) * half] += extra

    for copy in backs:
        copy.wait_recv()
    for copy in locals_[chunks:]:
        copy.wait()
    sent = infos + backs + stats + nears + fars
    for group in moves[1:] + pools + passes:
        sent = sent + group
    for copy in sent + z_copies:
        copy.wait_send()

    @pl.when(depth > 0)
    def _():
        for copy in t_copies:
            copy.wait_send()


def gradient_kernel(per, chunk_slots, target, lengths, returned, reduced, pooled, upstream, rows_out, pooled_gradient, weight_gradient):
    groups = returned.shape[0] // per
    block = groups * chunk_slots

    @pl.when(pl.program_id(0) == 0)
    def _():
        token = lax.broadcasted_iota(jnp.int32, returned.shape[1:], 0)

        def body(r, carry):
            p = target[r]
            rows_out[r] = jnp.where(token < lengths[r], returned[p], jnp.zeros_like(returned[p]))
            owner = p // per
            j = p % per
            row = j // chunk_slots * block + owner * chunk_slots + j % chunk_slots
            pooled_gradient[pl.ds(r, 1), :] = reduced[pl.ds(row, 1), :]
            return carry

        lax.fori_loop(0, rows_out.shape[0], body, 0)

    weight_gradient[...] = lax.dot_general(
        pooled[...], upstream[...], TN, preferred_element_type=jnp.float32
    )


def fused_shards(
    response_query,
    response_keys,
    prompt_cache,
    lengths,
    owners,
    pairing,
    residual,
    output_weight,
    norm_gain,
    reward_head,
):
    groups = lax.axis_size("dp")
    planes = lax.axis_size("mp")
    held_count, slot_count, width = response_query.shape
    local_heads = width // HD
    group_size = Q_HEADS // KV_HEADS
    per = held_count // groups
    count = held_count * groups
    columns = output_weight.shape[1]
    prefix = prompt_cache.shape[2]
    window = kv_window(planes, local_heads)
    chunk_slots = slots_of_chunk(groups, per)
    chunks = per // chunk_slots
    block = groups * chunk_slots
    chips = groups // 2
    span = window * HD
    packed_width = width + 2 * span
    bf16, f32 = jnp.bfloat16, jnp.float32
    vmem = pl.BlockSpec(memory_space=pltpu.VMEM)
    smem = pl.BlockSpec(memory_space=pltpu.SMEM)
    hbm = pl.BlockSpec(memory_space=pltpu.HBM)
    packed, info, target = pl.pallas_call(
        functools.partial(plan_kernel, per, chunk_slots, window),
        out_shape=(
            jax.ShapeDtypeStruct((held_count, slot_count, packed_width), bf16),
            jax.ShapeDtypeStruct((groups, 16, HD), f32),
            jax.ShapeDtypeStruct((held_count,), jnp.int32),
        ),
        in_specs=[smem, smem, hbm, hbm],
        out_specs=(vmem, vmem, smem),
        scratch_shapes=[
            pltpu.SMEM((groups,), jnp.int32),
            pltpu.VMEM((held_count, slot_count, width), bf16),
            pltpu.VMEM((2, held_count, slot_count, span), bf16),
            pltpu.SemaphoreType.DMA((3,)),
        ],
        compiler_params=pltpu.CompilerParams(vmem_limit_bytes=61 << 20),
        name="plan",
    )(owners, lengths, response_query, response_keys)
    slots = held_count * slot_count
    sub = SUB
    steps = count // sub
    halves = 2
    half = width // halves
    dma = lambda *shape: pltpu.SemaphoreType.DMA(shape)
    returned, pooled, upstream, reduced, head_gradient, rewards, loss = pl.pallas_call(
        functools.partial(
            layer_kernel, (groups, planes, per, chunk_slots, window, sub)
        ),
        out_shape=(
            jax.ShapeDtypeStruct((slots, width), bf16),
            jax.ShapeDtypeStruct((count, width), bf16),
            jax.ShapeDtypeStruct((count, columns), bf16),
            jax.ShapeDtypeStruct((held_count, width), f32),
            jax.ShapeDtypeStruct((1, columns), f32),
            jax.ShapeDtypeStruct((1, count), f32),
            jax.ShapeDtypeStruct((1, 1), f32),
        ),
        in_specs=[vmem, vmem, hbm, hbm, hbm, vmem, vmem, vmem],
        out_specs=(vmem,) * 7,
        scratch_shapes=[
            pltpu.VMEM((slots, packed_width), bf16),
            pltpu.VMEM((groups, 16, HD), f32),
            pltpu.VMEM((2, prefix, span), bf16),
            pltpu.VMEM((width, columns), bf16),
            pltpu.VMEM((count, columns), bf16),
            pltpu.VMEM((count, count), bf16),
            pltpu.VMEM((count // 2, count), f32),
            pltpu.VMEM((groups * block, groups * block), bf16),
            pltpu.VMEM((count, columns), f32),
            pltpu.VMEM((slots, width), bf16),
            pltpu.VMEM((count, columns), f32),
            pltpu.VMEM((count, columns), bf16),
            pltpu.VMEM((2, count, columns), bf16),
            pltpu.VMEM((count, columns), bf16),
            pltpu.VMEM((count, columns), f32),
            pltpu.VMEM((8, HD), f32),
            pltpu.VMEM((groups, 8, HD), f32),
            pltpu.VMEM((2, chips * held_count, columns), bf16),
            pltpu.VMEM((halves, chips * held_count, half), bf16),
            pltpu.VMEM((halves, chips * held_count, half), bf16),
            pltpu.VMEM((halves, chips - 1, held_count, half), bf16),
            pltpu.VMEM((halves, chips - 1, held_count, half), bf16),
            dma(4),
            dma(2, groups - 1),
            dma(2, chunks * (groups - 1)),
            dma(2 * chunks),
            dma(2, chunks * chips),
            dma(2, chunks * (chips - 1)),
            dma(2, chunks * (groups - 1)),
            dma(2, 2, steps),
            dma(2, steps),
            dma(2, groups - 1),
            dma(2, halves),
            dma(2, halves * (chips - 1)),
        ],
        compiler_params=pltpu.CompilerParams(
            collective_id=0, has_side_effects=True, vmem_limit_bytes=44 << 20
        ),
        name="layer",
    )(
        packed.reshape(slots, packed_width),
        info,
        prompt_cache,
        output_weight,
        residual,
        norm_gain[None],
        reward_head[None],
        pairing[None],
    )
    tile = 512
    attention_rows, pooled_gradient, weight_gradient = pl.pallas_call(
        functools.partial(gradient_kernel, per, chunk_slots),
        out_shape=(
            jax.ShapeDtypeStruct(response_query.shape, bf16),
            jax.ShapeDtypeStruct((held_count, width), f32),
            jax.ShapeDtypeStruct((width, columns), f32),
        ),
        grid=(width // tile,),
        in_specs=[
            smem,
            smem,
            pl.BlockSpec((held_count, slot_count, width), lambda i: (0, 0, 0)),
            pl.BlockSpec((held_count, width), lambda i: (0, 0)),
            pl.BlockSpec((count, tile), lambda i: (0, i)),
            pl.BlockSpec((count, columns), lambda i: (0, 0)),
        ],
        out_specs=(
            pl.BlockSpec((held_count, slot_count, width), lambda i: (0, 0, 0)),
            pl.BlockSpec((held_count, width), lambda i: (0, 0)),
            pl.BlockSpec((tile, columns), lambda i: (i, 0)),
        ),
        compiler_params=pltpu.CompilerParams(vmem_limit_bytes=32 << 20),
        name="gradient",
    )(
        target,
        lengths,
        returned.reshape(held_count, slot_count, width),
        reduced,
        pooled,
        upstream,
    )
    return (
        attention_rows,
        rewards[0],
        loss[0, 0],
        weight_gradient,
        head_gradient[0],
        pooled_gradient,
    )


SUB = 32


def kv_window(planes, local_heads):
    group_size = Q_HEADS // KV_HEADS
    return max(
        (m * local_heads + local_heads - 1) // group_size - m * local_heads // group_size + 1
        for m in range(planes)
    )


def slots_of_chunk(groups, per):
    for slots in range(1, per + 1):
        if per % slots == 0 and slots * groups % 16 == 0:
            return slots
    return 0


def fits(shape, responses):
    groups, planes = shape["dp"], shape["mp"]
    held = responses // groups
    if held % groups or groups % 2 or planes % 2:
        return False
    slots = slots_of_chunk(groups, held // groups)
    return bool(slots) and slots * groups * 8 == HD and responses % HD == 0 and responses <= 3 * HD


def shards(*args):
    held = args[0].shape[0]
    groups = lax.axis_size("dp")
    sizes = {"dp": groups, "mp": lax.axis_size("mp")}
    if fits(sizes, held * groups):
        return fused_shards(*args)
    return stepwise_shards(*args)


def solution(mesh):
    placed = (
        P("dp", None, "mp"),
        P(None, "dp", None, None),
        P(None, "dp", None, None),
        P("dp"),
        P("dp"),
        P(),
        P(None, "dp"),
        P("mp", "dp"),
        P("dp"),
        P("dp"),
    )
    return jax.shard_map(
        shards,
        mesh=mesh,
        in_specs=placed,
        out_specs=(P("dp", None, "mp"), P(), P(), P("mp", "dp"), P("dp"), P("dp", "mp")),
        check_vma=False,
    )
```
